128 devices in a mesh: dp: 16 (over x, y), red: 8 (over z, core).
Axes of the slice: x: 4, y: 4, z: 4, core: 2. Of those that a mesh axis runs over, the one named last changes fastest.
Arguments:
- frames: bfloat16 [2048, 48, 1536], P(('dp', 'red')), may hold values from -36 to 36
- cotangent: bfloat16 [2048, 48, 1536], P(('dp', 'red')), may hold values from -6 to 6
- w_in: bfloat16 [1536, 3072], P('red'), may hold values from -0.15625 to 0.15625
- kernel: float32 [31, 1536], replicated, may hold values from -1 to 1
- gain: float32 [1536], replicated, may hold values from 0.25 to 1.75
- lengths: int32 [2048], replicated, may hold values from 1 to 47, as said below
Outputs:
- module_output: bfloat16 [2048, 48, 1536], P(('dp', 'red'))
- frame_gradient: bfloat16 [2048, 48, 1536], P(('dp', 'red'))
- grad_w_in: float32 [1536, 3072], P('red')
- grad_kernel: float32 [31, 1536], replicated
- grad_gain: float32 [1536], replicated
The draws below stay inside these ranges and needn't reach their ends.
Inputs may be any that keep to these rules, and one draw needn't show every extreme that they name: The slots of each device, in order, form 16 groups of 1 slots. The q-th slot of group j on the device with dp index i and red index r and the q-th slot of group j on the device with dp index (2 j + 1 - i) mod 16 and the same red index have lengths that sum to exactly 48. The slots of dp index 0 all hold at least three quarters of 48 frames, rounded up.
All inputs are finite; a program needn't handle non-finite values.
Results may differ from the reference program's by a relative error of at most 0.0054.
Values may be sent and summed in bfloat16 or wider, within the bound.
A program may use at most 128 MiB of HBM per device.

```python
import math
import jax
import jax.numpy as jnp
from jax import lax

D = 1536
K = 31
UTT_DEV = 16
MAXLEN = 48
UTTS = 2048
N_DP = 16
N_RED = 8


def draw_frames(key, part):
    key_base, key_rows, key_cols = jax.random.split(key, 3)
    row_scales = jnp.exp(jax.random.uniform(key_rows, (UTTS, MAXLEN, 1), jnp.float32, math.log(0.3), math.log(3.0)))
    col_scales = jnp.exp(jax.random.uniform(key_cols, (D,), jnp.float32, math.log(0.3), math.log(3.0)))
    base_draw = jnp.clip(jax.random.normal(key_base, (UTTS, MAXLEN, D), jnp.float32), -4.0, 4.0)
    return (base_draw * row_scales * col_scales).astype(jnp.bfloat16)


def draw_lengths(key, part):
    per_peer = UTT_DEV // N_DP
    key_base, key_long = jax.random.split(jax.random.fold_in(key, 7))
    base_draw = jax.random.randint(key_base, (N_RED, N_DP, per_peer, N_DP), 1, MAXLEN)
    long_floor = (3 * MAXLEN + 3) // 4
    long_draw = jax.random.randint(key_long, (N_RED, N_DP, per_peer), long_floor, MAXLEN)
    long_draw = long_draw.at[:, 0, 0].set(MAXLEN - 1)
    source = jnp.arange(N_DP, dtype=jnp.int32)
    target = jnp.arange(N_DP, dtype=jnp.int32)
    partner = (2 * target[:, None] + 1 - source[None, :]) % N_DP
    lower = jnp.minimum(source[None, :], partner)
    lower_full = jnp.broadcast_to(lower[None, :, None, :], base_draw.shape)
    picked = jnp.take_along_axis(base_draw, lower_full, axis=3)
    chosen = jnp.where(lower_full == 0, long_draw[..., None], picked)
    length_grid = jnp.where(source[None, None, None, :] == lower_full, chosen, MAXLEN - chosen)
    return jnp.transpose(length_grid, (3, 0, 1, 2)).reshape(N_DP * N_RED * UTT_DEV).astype(jnp.int32)


def levels(rng, shape, shards, least, largest):
    level = 1.0
    for dim, blocks in shards:
        draws = jax.random.uniform(jax.random.fold_in(jax.random.fold_in(rng, 6), dim), (blocks,), jnp.float32, least / len(shards), largest / len(shards))
        level = level * jnp.repeat(jnp.exp(draws), shape[dim] // blocks).reshape((-1,) + (1,) * (len(shape) - 1 - dim))
    return level


def bell_draw(key, dims, scale, most, cuts=(), kind=jnp.bfloat16):
    result = scale * jax.random.normal(key, dims, jnp.float32)
    if cuts:
        result = result * levels(key, dims, cuts, -0.22, 0.18)
    return jnp.clip(result, -most, most).astype(kind)


def setup_inputs(seed: int = 0) -> dict:
    arg_keys = jax.random.split(jax.random.key(seed), 7)
    frames = draw_frames(jax.random.fold_in(arg_keys[6], 71), 0)
    cotangent = bell_draw(arg_keys[1], (UTTS, MAXLEN, D), 1.0, 6.0, ((0, 128),))
    w_in = bell_draw(arg_keys[2], (D, 2 * D), D ** -0.5, 0.15625, ((0, 8),))
    kernel = bell_draw(arg_keys[3], (K, D), K ** -0.5, 1.0, (), jnp.float32)
    gain = jnp.clip(1.0 + 0.15 * jax.random.normal(arg_keys[4], (D,), jnp.float32), 0.25, 1.75)
    lengths = draw_lengths(jax.random.fold_in(arg_keys[6], 71), 0)
    return dict(frames=frames, cotangent=cotangent, w_in=w_in, kernel=kernel, gain=gain, lengths=lengths)


EPSILON = 1e-05

def normalize(widened_frames):
    center = widened_frames - lax.optimization_barrier(jnp.mean(widened_frames, axis=-1, keepdims=True))
    inv_std = lax.rsqrt(lax.optimization_barrier(jnp.mean(center * center, axis=-1, keepdims=True)) + EPSILON)
    return (center * inv_std, inv_std)

def block_pass(frames, cotangent, valid_frame_mask, segment, weights, kernel, gain):
    row_count, length, model_width = frames.shape
    tap_count = kernel.shape[0]
    reach = tap_count // 2
    widened_frames = frames.astype(jnp.float32)
    normed, inv_std = normalize(widened_frames)
    scaled = (normed * gain).astype(jnp.bfloat16)
    flat_in = scaled.reshape(row_count * length, model_width)
    hidden = jnp.dot(flat_in, weights, preferred_element_type=jnp.float32)
    hidden = hidden.reshape(row_count, length, 2 * model_width)
    value_portion = hidden[..., :model_width]
    gate_sigmoid = jax.nn.sigmoid(hidden[..., model_width:])
    frame_validity = valid_frame_mask.astype(jnp.float32)[..., None]
    gated_linear_output = value_portion * gate_sigmoid * frame_validity
    padded = jnp.pad(gated_linear_output, ((0, 0), (reach, reach), (0, 0)))
    seg_pad = jnp.pad(segment, ((0, 0), (reach, reach)), constant_values=-1)
    convolved_frames = jnp.zeros_like(gated_linear_output)
    for offset in range(tap_count):
        window = padded[:, offset:offset + length]
        same_seg = (seg_pad[:, offset:offset + length] == segment).astype(jnp.float32)[..., None]
        convolved_frames = convolved_frames + kernel[offset] * (window * same_seg)
    swish_activation = jax.nn.sigmoid(convolved_frames)
    module_output = ((widened_frames + convolved_frames * swish_activation) * frame_validity).astype(jnp.bfloat16)
    incoming_gradient = cotangent.astype(jnp.float32) * frame_validity
    grad_conv = incoming_gradient * (swish_activation * (1.0 + convolved_frames * (1.0 - swish_activation)))
    grad_pad = jnp.pad(grad_conv, ((0, 0), (reach, reach), (0, 0)))
    gated_linear_gradient = jnp.zeros_like(gated_linear_output)
    kernel_terms = []
    for offset in range(tap_count):
        window = padded[:, offset:offset + length]
        same_seg = (seg_pad[:, offset:offset + length] == segment).astype(jnp.float32)[..., None]
        kernel_terms.append(lax.optimization_barrier(jnp.sum(grad_conv * window * same_seg, axis=(0, 1))))
        back_start = 2 * reach - offset
        back_same = (seg_pad[:, back_start:back_start + length] == segment).astype(jnp.float32)[..., None]
        gated_linear_gradient = gated_linear_gradient + kernel[offset] * (grad_pad[:, back_start:back_start + length] * back_same)
    gated_linear_gradient = gated_linear_gradient * frame_validity
    grad_hidden = jnp.concatenate([gated_linear_gradient * gate_sigmoid, gated_linear_gradient * value_portion * gate_sigmoid * (1.0 - gate_sigmoid)], axis=-1).astype(jnp.bfloat16)
    flat_grad = grad_hidden.reshape(row_count * length, 2 * model_width)
    grad_scaled = lax.dot_general(flat_grad, weights, (((1,), (1,)), ((), ())), preferred_element_type=jnp.float32)
    grad_scaled = grad_scaled.reshape(row_count, length, model_width)
    gain_term = lax.optimization_barrier(jnp.sum(grad_scaled * normed, axis=(0, 1)))
    grad_normed = grad_scaled * gain
    frame_gradient = incoming_gradient + inv_std * (grad_normed - lax.optimization_barrier(jnp.mean(grad_normed, axis=-1, keepdims=True)) - normed * lax.optimization_barrier(jnp.mean(grad_normed * normed, axis=-1, keepdims=True)))
    frame_gradient = (frame_gradient * frame_validity).astype(jnp.bfloat16)
    return (module_output, frame_gradient, flat_in, flat_grad, jnp.stack(kernel_terms), gain_term)

def reference(frames, cotangent, w_in, kernel, gain, lengths):
    positions = jnp.arange(MAXLEN, dtype=jnp.int32)
    blocks = UTTS // UTT_DEV

    def accumulate(totals, inputs):
        frame_block, cot_block, len_block = inputs
        valid_frame_mask = positions[None, :] < len_block[:, None]
        segment = jnp.where(valid_frame_mask, 0, 1).astype(jnp.int32)
        module_output, frame_gradient, flat_in, flat_grad, kernel_part, gain_part = block_pass(frame_block, cot_block, valid_frame_mask, segment, w_in, kernel, gain)
        weight_part = lax.dot_general(flat_in, flat_grad, (((0,), (0,)), ((), ())), preferred_element_type=jnp.float32)
        return ((totals[0] + weight_part, totals[1] + kernel_part, totals[2] + gain_part), (module_output, frame_gradient))
    initial = (jnp.zeros((D, 2 * D), jnp.float32), jnp.zeros((K, D), jnp.float32), jnp.zeros((D,), jnp.float32))
    totals_out, (outputs, gradients) = lax.scan(accumulate, initial, (frames.reshape(blocks, UTT_DEV, MAXLEN, D), cotangent.reshape(blocks, UTT_DEV, MAXLEN, D), lengths.reshape(blocks, UTT_DEV)))
    grad_scale = lax.rsqrt(jnp.sum(lengths).astype(jnp.float32))
    return (outputs.reshape(UTTS, MAXLEN, D), gradients.reshape(UTTS, MAXLEN, D), totals_out[0] * grad_scale, totals_out[1] * grad_scale, totals_out[2] * grad_scale)
```

```python
import functools

import jax
import jax.numpy as jnp
from jax import lax
from jax.experimental import pallas as pl
from jax.experimental.pallas import tpu as pltpu
from jax.sharding import PartitionSpec as P

EPSILON = 1e-05
D = 1536
K = 31
R = K // 2
U = 16
L = 48
N = U * L
C = 256
C2 = 2 * C
NB = D // C
LT = C // 128
T = 8
RB = 192
RX = RB // 4
MESH = pl.DeviceIdType.MESH
f32 = jnp.float32
bf16 = jnp.bfloat16


def sigmoid(x):
    return 0.5 * jnp.tanh(0.5 * x) + 0.5


def aligned(i, n):
    return pl.ds(pl.multiple_of(i, n), n)


def body(
    frames, cot, w, kern, gain, lens,
    mo_o, fg_o, gw_o, gk_o, gg_o,
    nat0, nat1, pm, pmt, fr, up, mean, istd, sc, sct, W, gh, h, glu, gcp, mot, kg, len16, gs,
    own, sibs, sibr, s1s, s1r, s2s, s2r, gwp,
    kgl, kgsr, kg1, kg1r, kg2, kg2r, kgo, ggl, ggr, gg2, gg2r, gg3, gg3r,
    in_sem, mo_sem, wl_sem, wz_s, wz_r, ws_s, ws_r,
    ss_s, ss_r, s1_s, s1_r, s2_s, s2_r, s3_s, s3_r, s3_l,
    ks_s, ks_r, k1_s, k1_r, k2_s, k2_r, k3_s, k3_r, g_s, g_r,
):
    dp, red = lax.axis_index("dp"), lax.axis_index("red")
    x, y = lax.div(dp, 4), lax.rem(dp, 4)
    z, c = lax.div(red, 2), lax.rem(red, 2)

    def turn(a, d):
        return lax.rem(a + d, 4)

    def at(ax, ay, az, ac):
        return (ax * 4 + ay, az * 2 + ac)

    sib = at(x, y, z, 1 - c)

    def remote(src, dst, ssem, rsem, dev):
        return pltpu.make_async_remote_copy(
            src_ref=src, dst_ref=dst, send_sem=ssem, recv_sem=rsem, device_id=dev, device_id_type=MESH
        )

    def first(b, d):
        p = lax.rem(b, 2)
        return at(turn(x, d * (1 - p)), turn(y, d * p), z, c)

    def plane(b, d, dz):
        p = lax.rem(b, 2)
        return at(turn(x, d * p), turn(y, d * (1 - p)), turn(z, dz), c)

    def place(b):
        p = lax.rem(b, 2)
        return x * (1 - p) + y * p, x * p + y * (1 - p)

    in0 = pltpu.make_async_copy(frames, nat0, in_sem.at[0])
    in0.start()

    def own_w(b, half):
        return pltpu.make_async_copy(
            w.at[:, aligned(half * D + b * C, C)], W.at[b, red, :, pl.ds(half * C, C)], wl_sem.at[b, half]
        )

    for b in range(NB):
        own_w(b, 0).start()
        own_w(b, 1).start()
    in1 = pltpu.make_async_copy(cot, nat1, in_sem.at[1])
    in1.start()

    barrier = pltpu.get_barrier_semaphore()
    offsets = [
        (i, j, k) for i in range(4) for j in range(4) for k in range(4) if (i, j, k) != (0, 0, 0) and i * j * k == 0
    ]
    pl.semaphore_signal(barrier, inc=1, device_id=sib, device_id_type=MESH)
    for i, j, k in offsets:
        pl.semaphore_signal(barrier, inc=1, device_id=at(turn(x, i), turn(y, j), turn(z, k), c), device_id_type=MESH)
    pl.semaphore_wait(barrier, len(offsets) + 1)

    def wz(b, j):
        return remote(W.at[b, red], W.at[b, red], wz_s.at[b, j - 1], wz_r.at[b, j - 1], at(x, y, turn(z, j), c))

    def wsib(b, j):
        held = turn(z, 4 - j) * 2 + c
        return remote(W.at[b, held], W.at[b, held], ws_s.at[b, j], ws_r.at[b, j], sib)

    def send_w(b, _):
        own_w(b, 0).wait()
        own_w(b, 1).wait()
        for j in (1, 3, 2):
            wz(b, j).start()
        wsib(b, 0).start()
        return 0

    def forward_w(b):
        for j in (1, 3, 2):
            wz(b, j).wait_recv()
            wsib(b, j).start()

    def arrived_w(b):
        for j in range(4):
            wsib(b, j).wait_recv()

    def sent_w(b, _):
        for j in (1, 2, 3):
            wz(b, j).wait_send()
        for j in range(4):
            wsib(b, j).wait_send()
        return 0

    lax.fori_loop(0, NB, send_w, 0)

    r0 = lax.broadcasted_iota(jnp.int32, (N, N), 0)
    r1 = lax.broadcasted_iota(jnp.int32, (N, N), 1)
    pm[...] = jnp.where(((r0 & 15) * L + (r0 >> 4)) == r1, 1.0, 0.0).astype(bf16)
    pmt[...] = jnp.where(((r1 & 15) * L + (r1 >> 4)) == r0, 1.0, 0.0).astype(bf16)
    me = dp * 8 + red
    row = lens[pl.ds(lax.div(me, 8), 1), :]
    sub = lax.broadcasted_iota(jnp.int32, (U, 128), 0)
    lane = lax.broadcasted_iota(jnp.int32, (U, 128), 1)
    mine = jnp.where(lane == sub + lax.rem(me, 8) * U, row, 0)
    len16[...] = jnp.broadcast_to(jnp.sum(mine, axis=1, keepdims=True), (U, 128))
    every = jnp.sum(jnp.sum(lens[...], axis=0, keepdims=True), axis=1, keepdims=True)
    root = lax.rsqrt(every.astype(f32))
    glu[...] = jnp.zeros_like(glu)
    gcp[...] = jnp.zeros_like(gcp)
    gg3[...] = jnp.zeros_like(gg3)

    def live(t0, n, lanes):
        t = lax.broadcasted_iota(jnp.int32, (n, U, lanes), 0) + t0
        return t < len16[:, :lanes][None]

    in0.wait()
    PR = 256

    def perm_frames(i, _):
        rows = aligned(i * PR, PR)
        fr[rows, :] = jnp.dot(pm[rows, :], nat0[...], preferred_element_type=f32).astype(bf16)
        return 0

    lax.fori_loop(0, N // PR, perm_frames, 0)

    def norm(i, _):
        NR = 128
        rows = aligned(i * NR, NR)
        v = fr[rows, :].astype(f32)
        m = jnp.mean(v, axis=-1, keepdims=True)
        cen = v - m
        s = lax.rsqrt(jnp.mean(cen * cen, axis=-1, keepdims=True) + EPSILON)
        mean[rows, :] = m
        istd[rows, :] = s
        scaled = cen * s * gain[...]
        sc[rows, :] = scaled.astype(bf16)
        turned = scaled.T.astype(bf16)
        for q in range(8):
            other = lax.rem(c + q % 2, 2)
            dst = other * (4 * RB) + (q // 2) * RB
            sct[aligned_rows(dst, RB), rows] = turned[q * RB : (q + 1) * RB, :]
        return 0

    def aligned_rows(i, n):
        return pl.ds(pl.multiple_of(i, 64), n)

    lax.fori_loop(0, N // 128, norm, 0)
    in1.wait()

    def perm_cot(i, _):
        rows = aligned(i * PR, PR)
        v = jnp.dot(pm[rows, :], nat1[...], preferred_element_type=f32).reshape(PR // U, U, D)
        up[rows, :] = jnp.where(live(i * (PR // U), PR // U, 1), v, 0.0).reshape(PR, D).astype(bf16)
        return 0

    lax.fori_loop(0, N // PR, perm_cot, 0)

    def sib_send(b):
        return remote(sibs.at[lax.rem(b, 2)], sibr.at[b], ss_s.at[lax.rem(b, 2)], ss_r.at[b], sib)

    def ksib(b):
        return remote(kgl.at[b], kgsr.at[b], ks_s.at[b], ks_r.at[b], sib)

    def s1(b, j):
        p = lax.rem(b, 2)
        f, _ = place(b)
        return remote(s1s.at[p, turn(f, j)], s1r.at[b, j - 1], s1_s.at[p, j - 1], s1_r.at[b, j - 1], first(b, j))

    def k1(b, j):
        f, _ = place(b)
        return remote(kg1.at[b, turn(f, j)], kg1r.at[b, j - 1], k1_s.at[b, j - 1], k1_r.at[b, j - 1], first(b, j))

    def s2(b, i):
        p = lax.rem(b, 2)
        _, s = place(b)
        d, dz = lax.div(i, 4), lax.rem(i, 4)
        return remote(
            s2s.at[p, turn(s, d), turn(z, dz)], s2r.at[b, i - 1], s2_s.at[p, i - 1], s2_r.at[b, i - 1], plane(b, d, dz)
        )

    def k2(b, i):
        d, dz = lax.div(i, 4), lax.rem(i, 4)
        return remote(kg2.at[b], kg2r.at[b, i - 1], k2_s.at[b, i - 1], k2_r.at[b, i - 1], plane(b, d, dz))

    def piece(b):
        f, s = place(b)
        return gw_o.at[aligned(f * RX, RX), aligned(lax.div(s, 2) * D + b * C + lax.rem(s, 2) * 128, 128)]

    def s3(b, i):
        dev = at(turn(x, lax.div(i, 4)), turn(y, lax.rem(i, 4)), z, c)
        return remote(gwp.at[b], piece(b), s3_s.at[b, i - 1], s3_r.at[b, i - 1], dev)

    def s3_own(b):
        return pltpu.make_async_copy(gwp.at[b], piece(b), s3_l.at[b])

    def k3(b, j):
        f, _ = place(b)
        return remote(kgo.at[b, f], kgo.at[b, f], k3_s.at[b, j - 1], k3_r.at[b, j - 1], first(b, j))

    def loop15(fn):
        def step(i, _):
            fn(i)
            return 0

        lax.fori_loop(1, 16, step, 0)

    def stage1(b):
        p = lax.rem(b, 2)
        sib_send(b).wait_recv()

        @pl.when(b >= 2)
        def _():
            for j in (1, 2, 3):
                s1(b - 2, j).wait_send()

        def add(q, _):
            v = own[q] + sibr[b, q].astype(f32)
            for f in range(4):
                s1s[p, f, q] = v[f * RX : (f + 1) * RX].astype(bf16)
            return 0

        lax.fori_loop(0, 4, add, 0)
        for j in (1, 3, 2):
            s1(b, j).start()
        ksib(b).wait_recv()
        t = kgl[b] + kgsr[b]
        for f in range(4):
            kg1[b, f] = t[f * 8 : (f + 1) * 8]
        for j in (1, 3, 2):
            k1(b, j).start()

    def stage2(b):
        p = lax.rem(b, 2)
        f, _ = place(b)
        for j in (1, 2, 3):
            s1(b, j).wait_recv()

        @pl.when(b >= 2)
        def _():
            loop15(lambda i: s2(b - 2, i).wait_send())

        def add(q, _):
            v = s1s[p, f, q].astype(f32)
            for j in range(3):
                v = v + s1r[b, j, q].astype(f32)
            for s in range(4):
                s2s[p, s, q] = v[:, s * 128 : (s + 1) * 128].astype(bf16)
            return 0

        lax.fori_loop(0, 4, add, 0)
        loop15(lambda i: s2(b, i).start())
        for j in (1, 2, 3):
            k1(b, j).wait_recv()
        kg2[b] = kg1[b, f] + kg1r[b, 0] + kg1r[b, 1] + kg1r[b, 2]
        loop15(lambda i: k2(b, i).start())

    def stage3(b):
        p = lax.rem(b, 2)
        f, s = place(b)
        loop15(lambda i: s2(b, i).wait_recv())
        v = s2s[p, s, z].astype(f32)
        for i in range(15):
            v = v + s2r[b, i].astype(f32)
        gwp[b] = (v * root).astype(bf16)
        loop15(lambda i: s3(b, i).start())
        s3_own(b).start()
        loop15(lambda i: k2(b, i).wait_recv())
        t = kg2[b]
        for i in range(15):
            t = t + kg2r[b, i]
        kgo[b, f] = t * root
        for j in (1, 2, 3):
            k3(b, j).start()

    def block(b, _):
        forward_first = b == 0

        @pl.when(forward_first)
        def _():
            forward_w(b)

        arrived_w(b)

        def hidden(i, _):
            rows = aligned(i * 256, 256)
            h[rows, :] = jnp.dot(sc[rows, :], W[b].reshape(D, C2), preferred_element_type=f32)
            return 0

        lax.fori_loop(0, N // 256, hidden, 0)

        @pl.when(b >= 1)
        def _():
            stage1(b - 1)

        for lt in range(LT):
            vl = slice(lt * 128, (lt + 1) * 128)
            gl = slice(C + lt * 128, C + (lt + 1) * 128)
            cl = aligned(b * C + lt * 128, 128)

            def gate(i, _):
                rows = aligned(i * (T * U), T * U)
                s = sigmoid(h[rows, gl])
                h[rows, gl] = s
                out = jnp.where(live(i * T, T, 128), (h[rows, vl] * s).reshape(T, U, 128), 0.0)
                glu[lt, pl.ds(i * T + R, T)] = out
                return 0

            lax.fori_loop(0, L // T, gate, 0)
            kg[...] = jnp.zeros_like(kg)

            def forward(i, _):
                t0 = i * T
                rows = aligned(i * (T * U), T * U)
                acc = jnp.zeros((T, U, 128), f32)
                for k in range(K):
                    acc = acc + kern[k : k + 1, cl][None] * glu[lt, pl.ds(t0 + k, T)]
                s = sigmoid(acc)
                swish = acc * s
                out = jnp.where(live(t0, T, 128), fr[rows, cl].astype(f32).reshape(T, U, 128) + swish, 0.0)
                mot[rows, vl] = out.reshape(T * U, 128).astype(bf16)
                gc = up[rows, cl].astype(f32).reshape(T, U, 128) * (s + swish * (1.0 - s))
                gcp[lt, pl.ds(t0 + R, T)] = gc
                for k in range(K):
                    p = jnp.sum(gc * glu[lt, pl.ds(t0 + k, T)], axis=0)
                    kg[k] += p[0:8] + p[8:16]
                return 0

            lax.fori_loop(0, L // T, forward, 0)
            kgl[b, :, vl] = jnp.sum(kg[...], axis=1)

            def backward(i, _):
                t0 = i * T
                rows = aligned(i * (T * U), T * U)
                acc = jnp.zeros((T, U, 128), f32)
                for k in range(K):
                    acc = acc + kern[k : k + 1, cl][None] * gcp[lt, pl.ds(t0 + (K - 1) - k, T)]
                dg = jnp.where(live(t0, T, 128), acc, 0.0)
                s = h[rows, gl].reshape(T, U, 128)
                gh[b, rows, vl] = (dg * s).reshape(T * U, 128).astype(bf16)
                gate_part = dg * glu[lt, pl.ds(t0 + R, T)] * (1.0 - s)
                gh[b, rows, gl] = gate_part.reshape(T * U, 128).astype(bf16)
                return 0

            lax.fori_loop(0, L // T, backward, 0)

        @pl.when(b + 1 < NB)
        def _():
            forward_w(b + 1)

        @pl.when(b >= 2)
        def _():
            sib_send(b - 2).wait_send()

        def dw_other(i, _):
            rows = aligned(i * 2 * RB + 4 * RB, 2 * RB)
            g = jnp.dot(sct[rows, :], gh[b], preferred_element_type=f32).astype(bf16)
            sibs[lax.rem(b, 2), pl.ds(2 * i, 2)] = g.reshape(2, RB, C2)
            return 0

        lax.fori_loop(0, 2, dw_other, 0)
        sib_send(b).start()
        ksib(b).start()

        def dw_own(i, _):
            rows = aligned(i * 2 * RB, 2 * RB)
            g = jnp.dot(sct[rows, :], gh[b], preferred_element_type=f32)
            own[pl.ds(2 * i, 2)] = g.reshape(2, RB, C2)
            return 0

        lax.fori_loop(0, 2, dw_own, 0)

        @pl.when(b >= 3)
        def _():
            stage3(b - 3)

        @pl.when(b >= 2)
        def _():
            stage2(b - 2)

        cols = aligned(b * C, C)

        def perm_out(i, _):
            rows = aligned(i * PR, PR)
            nat0[rows, cols] = jnp.dot(pmt[rows, :], mot[...], preferred_element_type=f32).astype(bf16)
            return 0

        lax.fori_loop(0, N // PR, perm_out, 0)
        mo_copy(b).start()
        return 0

    def mo_copy(b):
        cols = aligned(b * C, C)
        return pltpu.make_async_copy(nat0.at[:, cols], mo_o.at[:, cols], mo_sem.at[b])

    lax.fori_loop(0, NB, block, 0)

    stage3(NB - 3)
    stage2(NB - 2)
    stage1(NB - 1)
    ggl[...] = jnp.zeros_like(ggl)
    FR = 256

    def final(i, _):
        rows = aligned(i * FR, FR)

        def acc(b, _):
            p = lax.dot_general(
                gh[b, rows, :], W[b].reshape(D, C2), (((1,), (1,)), ((), ())), preferred_element_type=f32
            )

            @pl.when(b == 0)
            def _():
                gs[...] = p

            @pl.when(b > 0)
            def _():
                gs[...] += p

            return 0

        lax.fori_loop(0, NB, acc, 0)

        @pl.when(i == 1)
        def _():
            stage3(NB - 2)

        @pl.when(i == 2)
        def _():
            stage2(NB - 1)

        def ln(j, _):
            NR = 64
            part = aligned(j * NR, NR)
            r = pl.ds(pl.multiple_of(i * FR + j * NR, NR), NR)
            g0 = gs[part, :]
            s = istd[r, :]
            nm = (fr[r, :].astype(f32) - mean[r, :]) * s
            ggl[...] += jnp.sum((g0 * nm).reshape(NR // 8, 8, D), axis=0)
            g = g0 * gain[...]
            m1 = jnp.mean(g, axis=-1, keepdims=True)
            m2 = jnp.mean(g * nm, axis=-1, keepdims=True)
            o = up[r, :].astype(f32) + s * (g - m1 - nm * m2)
            lv = live(i * (FR // U) + j * (NR // U), NR // U, 1)
            nat1[r, :] = jnp.where(lv, o.reshape(NR // U, U, D), 0.0).reshape(NR, D).astype(bf16)
            return 0

        lax.fori_loop(0, FR // 64, ln, 0)
        return 0

    lax.fori_loop(0, N // FR, final, 0)

    total = jnp.sum(ggl[...], axis=0, keepdims=True)
    for q in range(D // 128):
        gg3[q : q + 1, :] = total[:, q * 128 : (q + 1) * 128]

    def g1():
        return remote(gg3, ggr, g_s.at[18], g_r.at[18], sib)

    def g2(i):
        return remote(gg2, gg2r.at[i - 1], g_s.at[i - 1], g_r.at[i - 1], plane(0, lax.div(i, 4), lax.rem(i, 4)))

    def g3(j):
        return remote(ggl2, gg3r.at[j - 1], g_s.at[14 + j], g_r.at[14 + j], first(0, j))

    ggl2 = ggl.at[:, 0:256]
    g1().start()

    def mo_done(b, _):
        mo_copy(b).wait()
        return 0

    lax.fori_loop(0, NB, mo_done, 0)

    def perm_grad(i, _):
        rows = aligned(i * PR, PR)
        nat0[rows, :] = jnp.dot(pmt[rows, :], nat1[...], preferred_element_type=f32).astype(bf16)
        return 0

    g1().wait_recv()
    gg2[...] = gg3[...] + ggr[...]
    loop15(lambda i: g2(i).start())
    stage3(NB - 1)
    lax.fori_loop(0, N // PR, perm_grad, 0)
    fg_copy = pltpu.make_async_copy(nat0, fg_o, in_sem.at[0])
    fg_copy.start()
    loop15(lambda i: g2(i).wait_recv())
    t = gg2[...]
    for i in range(15):
        t = t + gg2r[i]
    ggl[:, 0:128] = t[0:8]
    ggl[:, 128:256] = t[8:16]
    for j in (1, 2, 3):
        g3(j).start()

    def done(b, _):
        loop15(lambda i: s3(b, i).wait())
        s3_own(b).wait()
        for j in (1, 2, 3):
            k3(b, j).wait()
            k1(b, j).wait_send()
        ksib(b).wait_send()
        loop15(lambda i: k2(b, i).wait_send())
        gk_o[:, aligned(b * C, C)] = kgo[b].reshape(32, C)[0:K]
        return 0

    lax.fori_loop(0, NB, done, 0)
    lax.fori_loop(0, NB, sent_w, 0)
    for b in (NB - 2, NB - 1):
        sib_send(b).wait_send()
        for j in (1, 2, 3):
            s1(b, j).wait_send()
        loop15(lambda i: s2(b, i).wait_send())
    g1().wait_send()
    loop15(lambda i: g2(i).wait_send())
    for j in (1, 2, 3):
        g3(j).wait()
    t = (ggl[:, 0:256] + gg3r[0] + gg3r[1] + gg3r[2]) * root
    for q in range(D // 128):
        gg_o[0:1, q * 128 : (q + 1) * 128] = t[q % 8 : q % 8 + 1, (q // 8) * 128 : (q // 8 + 1) * 128]
    fg_copy.wait()


def local(frames, cotangent, w_in, kernel, gain, lengths):
    V, DMA = pltpu.VMEM, pltpu.SemaphoreType.DMA
    far = pl.BlockSpec(memory_space=pl.ANY)
    near = pl.BlockSpec(memory_space=pltpu.VMEM)
    mo, fg, gw, gk, gg = pl.pallas_call(
        body,
        out_shape=[
            jax.ShapeDtypeStruct((N, D), bf16),
            jax.ShapeDtypeStruct((N, D), bf16),
            jax.ShapeDtypeStruct((RB, 2 * D), bf16),
            jax.ShapeDtypeStruct((K, D), f32),
            jax.ShapeDtypeStruct((1, D), f32),
        ],
        in_specs=[far, far, far, near, near, near],
        out_specs=[far, far, far, near, near],
        scratch_shapes=[
            V((N, D), bf16), V((N, D), bf16), V((N, N), bf16), V((N, N), bf16), V((N, D), bf16), V((N, D), bf16),
            V((N, 1), f32), V((N, 1), f32), V((N, D), bf16), V((D, N), bf16),
            V((NB, 8, RB, C2), bf16), V((NB, N, C2), bf16), V((N, C2), f32),
            V((LT, L + 2 * R, U, 128), f32), V((LT, L + 2 * R, U, 128), f32), V((N, C), bf16),
            V((K + 1, 8, 128), f32), V((U, 128), jnp.int32), V((256, D), f32),
            V((4, RB, C2), f32), V((2, 4, RB, C2), bf16), V((NB, 4, RB, C2), bf16),
            V((2, 4, 4, RX, C2), bf16), V((NB, 3, 4, RX, C2), bf16),
            V((2, 4, 4, RX, 128), bf16), V((NB, 15, RX, 128), bf16), V((NB, RX, 128), bf16),
            V((NB, 32, C), f32), V((NB, 32, C), f32), V((NB, 4, 8, C), f32), V((NB, 3, 8, C), f32),
            V((NB, 8, C), f32), V((NB, 15, 8, C), f32), V((NB, 4, 8, C), f32),
            V((8, D), f32), V((16, 128), f32), V((16, 128), f32), V((15, 16, 128), f32),
            V((16, 128), f32), V((3, 8, 256), f32),
            DMA((2,)), DMA((NB,)), DMA((NB, 2)), DMA((NB, 3)), DMA((NB, 3)), DMA((NB, 4)), DMA((NB, 4)),
            DMA((2,)), DMA((NB,)), DMA((2, 3)), DMA((NB, 3)), DMA((2, 15)), DMA((NB, 15)),
            DMA((NB, 15)), DMA((NB, 15)), DMA((NB,)),
            DMA((NB,)), DMA((NB,)), DMA((NB, 3)), DMA((NB, 3)), DMA((NB, 15)), DMA((NB, 15)),
            DMA((NB, 3)), DMA((NB, 3)), DMA((19,)), DMA((19,)),
        ],
        compiler_params=pltpu.CompilerParams(collective_id=0, has_side_effects=True, vmem_limit_bytes=62 << 20),
    )(
        frames.reshape(N, D),
        cotangent.reshape(N, D),
        w_in,
        kernel,
        gain.reshape(1, D),
        lengths.reshape(16, 128),
    )
    return mo.reshape(U, L, D), fg.reshape(U, L, D), gw.astype(f32), gk, gg.reshape(D)


def solution(mesh):
    rows = P(("dp", "red"), None, None)
    return jax.shard_map(
        local,
        mesh=mesh,
        in_specs=(rows, rows, P("red", None), P(), P(), P()),
        out_specs=(rows, rows, P("red", None), P(), P()),
        check_vma=False,
    )
```

```python
import functools

import jax
import jax.numpy as jnp
from jax import lax
from jax.experimental import pallas as pl
from jax.experimental.pallas import tpu as pltpu
from jax.sharding import PartitionSpec as P

EPSILON = 1e-05
D = 1536
K = 31
R = K // 2
U = 16
L = 48
N = U * L
C = 256
C2 = 2 * C
NB = D // C
LT = C // 128
T = 8
RB = 192
RX = RB // 4
MESH = pl.DeviceIdType.MESH
f32 = jnp.float32
bf16 = jnp.bfloat16


def sigmoid(x):
    return 0.5 * jnp.tanh(0.5 * x) + 0.5


def aligned(i, n):
    return pl.ds(pl.multiple_of(i, n), n)


def body(
    frames, cot, w, kern, gain, lens,
    mo_o, fg_o, gw_o, gk_o, gg_o,
    nat0, nat1, pm, pmt, fr, up, mean, istd, sc, sct, W, gh, h, glu, gcp, mot, kg, len16, gs,
    own, sibs, sibr, s1s, s1r, s2s, s2r, gwp,
    kgl, kgsr, kg1, kg1r, kg2, kg2r, kgo, ggl, ggr, gg2, gg2r, gg3, gg3r, gg4,
    in_sem, mo_sem, wl_sem, wz_s, wz_r, ws_s, ws_r,
    ss_s, ss_r, s1_s, s1_r, s2_s, s2_r, s3_s, s3_r, s3_l,
    ks_s, ks_r, k1_s, k1_r, k2_s, k2_r, k3_s, k3_r, g_s, g_r,
):
    dp, red = lax.axis_index("dp"), lax.axis_index("red")
    x, y = lax.div(dp, 4), lax.rem(dp, 4)
    z, c = lax.div(red, 2), lax.rem(red, 2)

    def turn(a, d):
        return lax.rem(a + d, 4)

    def at(ax, ay, az, ac):
        return (ax * 4 + ay, az * 2 + ac)

    sib = at(x, y, z, 1 - c)

    def remote(src, dst, ssem, rsem, dev):
        return pltpu.make_async_remote_copy(
            src_ref=src, dst_ref=dst, send_sem=ssem, recv_sem=rsem, device_id=dev, device_id_type=MESH
        )

    def first(b, d):
        p = lax.rem(b, 2)
        return at(turn(x, d * (1 - p)), turn(y, d * p), z, c)

    def plane(b, d, dz):
        p = lax.rem(b, 2)
        return at(turn(x, d * p), turn(y, d * (1 - p)), turn(z, dz), c)

    def place(b):
        p = lax.rem(b, 2)
        return x * (1 - p) + y * p, x * p + y * (1 - p)

    in0 = pltpu.make_async_copy(frames, nat0, in_sem.at[0])
    in0.start()

    def own_w(b, half):
        return pltpu.make_async_copy(
            w.at[:, aligned(half * D + b * C, C)], W.at[b, red, :, pl.ds(half * C, C)], wl_sem.at[b, half]
        )

    for b in range(NB):
        own_w(b, 0).start()
        own_w(b, 1).start()
    in1 = pltpu.make_async_copy(cot, nat1, in_sem.at[1])
    in1.start()

    barrier = pltpu.get_barrier_semaphore()
    offsets = [
        (i, j, k) for i in range(4) for j in range(4) for k in range(4) if (i, j, k) != (0, 0, 0) and i * j * k == 0
    ]
    pl.semaphore_signal(barrier, inc=1, device_id=sib, device_id_type=MESH)
    for i, j, k in offsets:
        pl.semaphore_signal(barrier, inc=1, device_id=at(turn(x, i), turn(y, j), turn(z, k), c), device_id_type=MESH)
    pl.semaphore_wait(barrier, len(offsets) + 1)

    def wz(b, j):
        return remote(W.at[b, red], W.at[b, red], wz_s.at[b, j - 1], wz_r.at[b, j - 1], at(x, y, turn(z, j), c))

    def wsib(b, j):
        held = turn(z, 4 - j) * 2 + c
        return remote(W.at[b, held], W.at[b, held], ws_s.at[b, j], ws_r.at[b, j], sib)

    def send_w(b, _):
        own_w(b, 0).wait()
        own_w(b, 1).wait()
        for j in (1, 3, 2):
            wz(b, j).start()
        wsib(b, 0).start()
        return 0

    def forward_w(b):
        for j in (1, 3, 2):
            wz(b, j).wait_recv()
            wsib(b, j).start()

    def arrived_w(b):
        for j in range(4):
            wsib(b, j).wait_recv()

    def sent_w(b, _):
        for j in (1, 2, 3):
            wz(b, j).wait_send()
        for j in range(4):
            wsib(b, j).wait_send()
        return 0

    lax.fori_loop(0, NB, send_w, 0)

    r0 = lax.broadcasted_iota(jnp.int32, (N, N), 0)
    r1 = lax.broadcasted_iota(jnp.int32, (N, N), 1)
    pm[...] = jnp.where(((r0 & 15) * L + (r0 >> 4)) == r1, 1.0, 0.0).astype(bf16)
    pmt[...] = jnp.where(((r1 & 15) * L + (r1 >> 4)) == r0, 1.0, 0.0).astype(bf16)
    me = dp * 8 + red
    row = lens[pl.ds(lax.div(me, 8), 1), :]
    sub = lax.broadcasted_iota(jnp.int32, (U, 128), 0)
    lane = lax.broadcasted_iota(jnp.int32, (U, 128), 1)
    mine = jnp.where(lane == sub + lax.rem(me, 8) * U, row, 0)
    len16[...] = jnp.broadcast_to(jnp.sum(mine, axis=1, keepdims=True), (U, 128))
    every = jnp.sum(jnp.sum(lens[...], axis=0, keepdims=True), axis=1, keepdims=True)
    root = lax.rsqrt(every.astype(f32))
    glu[...] = jnp.zeros_like(glu)
    gcp[...] = jnp.zeros_like(gcp)
    gg3[...] = jnp.zeros_like(gg3)

    def live(t0, n, lanes):
        t = lax.broadcasted_iota(jnp.int32, (n, U, lanes), 0) + t0
        return t < len16[:, :lanes][None]

    in0.wait()
    PR = 256

    def perm_frames(i, _):
        rows = aligned(i * PR, PR)
        fr[rows, :] = jnp.dot(pm[rows, :], nat0[...], preferred_element_type=f32).astype(bf16)
        return 0

    lax.fori_loop(0, N // PR, perm_frames, 0)

    gain_row = jnp.concatenate([gain[q : q + 1, :] for q in range(D // 128)], axis=1)

    def norm(i, _):
        NR = 128
        rows = aligned(i * NR, NR)
        v = fr[rows, :].astype(f32)
        m = jnp.mean(v, axis=-1, keepdims=True)
        cen = v - m
        s = lax.rsqrt(jnp.mean(cen * cen, axis=-1, keepdims=True) + EPSILON)
        mean[rows, :] = m
        istd[rows, :] = s
        scaled = cen * s * gain_row
        sc[rows, :] = scaled.astype(bf16)
        turned = scaled.T.astype(bf16)
        for q in range(8):
            other = lax.rem(c + q % 2, 2)
            dst = other * (4 * RB) + (q // 2) * RB
            sct[aligned_rows(dst, RB), rows] = turned[q * RB : (q + 1) * RB, :]
        return 0

    def aligned_rows(i, n):
        return pl.ds(pl.multiple_of(i, 64), n)

    lax.fori_loop(0, N // 128, norm, 0)
    in1.wait()

    def perm_cot(i, _):
        rows = aligned(i * PR, PR)
        v = jnp.dot(pm[rows, :], nat1[...], preferred_element_type=f32).reshape(PR // U, U, D)
        up[rows, :] = jnp.where(live(i * (PR // U), PR // U, 1), v, 0.0).reshape(PR, D).astype(bf16)
        return 0

    lax.fori_loop(0, N // PR, perm_cot, 0)

    def sib_send(b):
        return remote(sibs.at[lax.rem(b, 2)], sibr.at[b], ss_s.at[lax.rem(b, 2)], ss_r.at[b], sib)

    def ksib(b):
        return remote(kgl.at[b], kgsr.at[b], ks_s.at[b], ks_r.at[b], sib)

    def s1(b, j):
        p = lax.rem(b, 2)
        f, _ = place(b)
        return remote(s1s.at[p, turn(f, j)], s1r.at[b, j - 1], s1_s.at[p, j - 1], s1_r.at[b, j - 1], first(b, j))

    def k1(b, j):
        f, _ = place(b)
        return remote(kg1.at[b, turn(f, j)], kg1r.at[b, j - 1], k1_s.at[b, j - 1], k1_r.at[b, j - 1], first(b, j))

    def s2(b, i):
        p = lax.rem(b, 2)
        _, s = place(b)
        d, dz = lax.div(i, 4), lax.rem(i, 4)
        return remote(
            s2s.at[p, turn(s, d), turn(z, dz)], s2r.at[b, i - 1], s2_s.at[p, i - 1], s2_r.at[b, i - 1], plane(b, d, dz)
        )

    def k2(b, i):
        d, dz = lax.div(i, 4), lax.rem(i, 4)
        return remote(kg2.at[b], kg2r.at[b, i - 1], k2_s.at[b, i - 1], k2_r.at[b, i - 1], plane(b, d, dz))

    def piece(b):
        f, s = place(b)
        return gw_o.at[aligned(f * RX, RX), aligned(lax.div(s, 2) * D + b * C + lax.rem(s, 2) * 128, 128)]

    def s3(b, i):
        dev = at(turn(x, lax.div(i, 4)), turn(y, lax.rem(i, 4)), z, c)
        return remote(gwp.at[b], piece(b), s3_s.at[b, i - 1], s3_r.at[b, i - 1], dev)

    def s3_own(b):
        return pltpu.make_async_copy(gwp.at[b], piece(b), s3_l.at[b])

    def k3(b, j):
        f, _ = place(b)
        return remote(kgo.at[b, f], kgo.at[b, f], k3_s.at[b, j - 1], k3_r.at[b, j - 1], first(b, j))

    def loop15(fn):
        def step(i, _):
            fn(i)
            return 0

        lax.fori_loop(1, 16, step, 0)

    def stage1(b):
        p = lax.rem(b, 2)
        sib_send(b).wait_recv()

        @pl.when(b >= 2)
        def _():
            for j in (1, 2, 3):
                s1(b - 2, j).wait_send()

        def add(q, _):
            v = own[q] + sibr[b, q].astype(f32)
            for f in range(4):
                s1s[p, f, q] = v[f * RX : (f + 1) * RX].astype(bf16)
            return 0

        lax.fori_loop(0, 4, add, 0)
        for j in (1, 3, 2):
            s1(b, j).start()
        ksib(b).wait_recv()
        t = kgl[b] + kgsr[b]
        for f in range(4):
            kg1[b, f] = t[f * 8 : (f + 1) * 8]
        for j in (1, 3, 2):
            k1(b, j).start()

    def stage2(b):
        p = lax.rem(b, 2)
        f, _ = place(b)
        for j in (1, 2, 3):
            s1(b, j).wait_recv()

        @pl.when(b >= 2)
        def _():
            loop15(lambda i: s2(b - 2, i).wait_send())

        def add(q, _):
            v = s1s[p, f, q].astype(f32)
            for j in range(3):
                v = v + s1r[b, j, q].astype(f32)
            for s in range(4):
                s2s[p, s, q] = v[:, s * 128 : (s + 1) * 128].astype(bf16)
            return 0

        lax.fori_loop(0, 4, add, 0)
        loop15(lambda i: s2(b, i).start())
        for j in (1, 2, 3):
            k1(b, j).wait_recv()
        kg2[b] = kg1[b, f] + kg1r[b, 0] + kg1r[b, 1] + kg1r[b, 2]
        loop15(lambda i: k2(b, i).start())

    def stage3(b):
        p = lax.rem(b, 2)
        f, s = place(b)
        loop15(lambda i: s2(b, i).wait_recv())
        v = s2s[p, s, z].astype(f32)
        for i in range(15):
            v = v + s2r[b, i].astype(f32)
        gwp[b] = (v * root).astype(bf16)
        loop15(lambda i: s3(b, i).start())
        s3_own(b).start()
        loop15(lambda i: k2(b, i).wait_recv())
        t = kg2[b]
        for i in range(15):
            t = t + kg2r[b, i]
        kgo[b, f] = t * root
        for j in (1, 2, 3):
            k3(b, j).start()

    def block(b, _):
        forward_first = b == 0

        @pl.when(forward_first)
        def _():
            forward_w(b)

        arrived_w(b)

        h[...] = jnp.dot(sc[...], W[b].reshape(D, C2), preferred_element_type=f32)

        @pl.when(b >= 1)
        def _():
            stage1(b - 1)

        for lt in range(LT):
            vl = slice(lt * 128, (lt + 1) * 128)
            gl = slice(C + lt * 128, C + (lt + 1) * 128)
            cl = aligned(b * C + lt * 128, 128)

            def gate(i, _):
                rows = aligned(i * (T * U), T * U)
                s = sigmoid(h[rows, gl])
                h[rows, gl] = s
                out = jnp.where(live(i * T, T, 128), (h[rows, vl] * s).reshape(T, U, 128), 0.0)
                glu[lt, pl.ds(i * T + R, T)] = out
                return 0

            lax.fori_loop(0, L // T, gate, 0)
            kg[...] = jnp.zeros_like(kg)

            def forward(i, _):
                t0 = i * T
                rows = aligned(i * (T * U), T * U)
                acc = jnp.zeros((T, U, 128), f32)
                for k in range(K):
                    acc = acc + kern[k : k + 1, cl][None] * glu[lt, pl.ds(t0 + k, T)]
                s = sigmoid(acc)
                swish = acc * s
                out = jnp.where(live(t0, T, 128), fr[rows, cl].astype(f32).reshape(T, U, 128) + swish, 0.0)
                mot[rows, vl] = out.reshape(T * U, 128).astype(bf16)
                gc = up[rows, cl].astype(f32).reshape(T, U, 128) * (s + swish * (1.0 - s))
                gcp[lt, pl.ds(t0 + R, T)] = gc
                for k in range(K):
                    p = jnp.sum(gc * glu[lt, pl.ds(t0 + k, T)], axis=0)
                    kg[k] += p[0:8] + p[8:16]
                return 0

            lax.fori_loop(0, L // T, forward, 0)
            kgl[b, :, vl] = jnp.sum(kg[...], axis=1)

            def backward(i, _):
                t0 = i * T
                rows = aligned(i * (T * U), T * U)
                acc = jnp.zeros((T, U, 128), f32)
                for k in range(K):
                    acc = acc + kern[k : k + 1, cl][None] * gcp[lt, pl.ds(t0 + (K - 1) - k, T)]
                dg = jnp.where(live(t0, T, 128), acc, 0.0)
                s = h[rows, gl].reshape(T, U, 128)
                gh[b, rows, vl] = (dg * s).reshape(T * U, 128).astype(bf16)
                gate_part = dg * glu[lt, pl.ds(t0 + R, T)] * (1.0 - s)
                gh[b, rows, gl] = gate_part.reshape(T * U, 128).astype(bf16)
                return 0

            lax.fori_loop(0, L // T, backward, 0)

        @pl.when(b + 1 < NB)
        def _():
            forward_w(b + 1)

        @pl.when(b >= 2)
        def _():
            sib_send(b - 2).wait_send()

        g = jnp.dot(sct[4 * RB :, :], gh[b], preferred_element_type=f32).astype(bf16)
        sibs[lax.rem(b, 2)] = g.reshape(4, RB, C2)
        sib_send(b).start()
        ksib(b).start()

        own[...] = jnp.dot(sct[: 4 * RB, :], gh[b], preferred_element_type=f32).reshape(4, RB, C2)

        @pl.when(b >= 3)
        def _():
            stage3(b - 3)

        @pl.when(b >= 2)
        def _():
            stage2(b - 2)

        cols = aligned(b * C, C)

        nat0[:, cols] = jnp.dot(pmt[...], mot[...], preferred_element_type=f32).astype(bf16)
        mo_copy(b).start()
        return 0

    def mo_copy(b):
        cols = aligned(b * C, C)
        return pltpu.make_async_copy(nat0.at[:, cols], mo_o.at[:, cols], mo_sem.at[b])

    lax.fori_loop(0, NB, block, 0)

    stage3(NB - 3)
    stage2(NB - 2)
    stage1(NB - 1)
    ggl[...] = jnp.zeros_like(ggl)

    def g1():
        return remote(gg3, ggr, g_s.at[18], g_r.at[18], sib)

    def g2(i):
        return remote(gg2, gg2r.at[i - 1], g_s.at[i - 1], g_r.at[i - 1], plane(0, lax.div(i, 4), lax.rem(i, 4)))

    def g3(j):
        return remote(gg4, gg3r.at[j - 1], g_s.at[14 + j], g_r.at[14 + j], first(0, j))

    def acc(b, _):
        p = lax.dot_general(gh[b], W[b].reshape(D, C2), (((1,), (1,)), ((), ())), preferred_element_type=f32)

        @pl.when(b == 0)
        def _():
            gs[...] = p

        @pl.when(b > 0)
        def _():
            gs[...] += p

        @pl.when(b == 4)
        def _():
            stage3(NB - 2)

        return 0

    lax.fori_loop(0, NB, acc, 0)
    NR = 64

    def normed(r):
        return (fr[r, :].astype(f32) - mean[r, :]) * istd[r, :]

    def gain_part(j, _):
        r = aligned(j * NR, NR)
        ggl[...] += jnp.sum((gs[r, :] * normed(r)).reshape(NR // 8, 8, D), axis=0)
        return 0

    lax.fori_loop(0, N // NR, gain_part, 0)
    total = jnp.sum(ggl[...], axis=0, keepdims=True)
    for q in range(D // 128):
        gg3[q : q + 1, :] = total[:, q * 128 : (q + 1) * 128]
    g1().start()

    def ln(j, _):
        @pl.when(j == 3)
        def _():
            g1().wait_recv()
            gg2[...] = gg3[...] + ggr[...]
            loop15(lambda i: g2(i).start())

        @pl.when(j == 7)
        def _():
            stage2(NB - 1)

        r = aligned(j * NR, NR)
        s = istd[r, :]
        nm = normed(r)
        g = gs[r, :] * gain_row
        m1 = jnp.mean(g, axis=-1, keepdims=True)
        m2 = jnp.mean(g * nm, axis=-1, keepdims=True)
        o = up[r, :].astype(f32) + s * (g - m1 - nm * m2)
        lv = live(j * (NR // U), NR // U, 1)
        nat1[r, :] = jnp.where(lv, o.reshape(NR // U, U, D), 0.0).reshape(NR, D).astype(bf16)
        return 0

    lax.fori_loop(0, N // NR, ln, 0)

    def mo_done(b, _):
        mo_copy(b).wait()
        return 0

    lax.fori_loop(0, NB, mo_done, 0)
    nat0[...] = jnp.dot(pmt[...], nat1[...], preferred_element_type=f32).astype(bf16)
    fg_copy = pltpu.make_async_copy(nat0, fg_o, in_sem.at[0])
    fg_copy.start()
    loop15(lambda i: g2(i).wait_recv())
    t = gg2[...]
    for i in range(15):
        t = t + gg2r[i]
    gg4[...] = t
    for j in (1, 2, 3):
        g3(j).start()
    stage3(NB - 1)

    def done(b, _):
        loop15(lambda i: s3(b, i).wait())
        s3_own(b).wait()
        for j in (1, 2, 3):
            k3(b, j).wait()
            k1(b, j).wait_send()
        ksib(b).wait_send()
        loop15(lambda i: k2(b, i).wait_send())
        gk_o[:, aligned(b * C, C)] = kgo[b].reshape(32, C)[0:K]
        return 0

    lax.fori_loop(0, NB, done, 0)
    lax.fori_loop(0, NB, sent_w, 0)
    for b in (NB - 2, NB - 1):
        sib_send(b).wait_send()
        for j in (1, 2, 3):
            s1(b, j).wait_send()
        loop15(lambda i: s2(b, i).wait_send())
    g1().wait_send()
    loop15(lambda i: g2(i).wait_send())
    for j in (1, 2, 3):
        g3(j).wait()
    gg_o[...] = ((gg4[...] + gg3r[0] + gg3r[1] + gg3r[2]) * root)[0 : D // 128]
    fg_copy.wait()


def local(frames, cotangent, w_in, kernel, gain, lengths):
    V, DMA = pltpu.VMEM, pltpu.SemaphoreType.DMA
    far = pl.BlockSpec(memory_space=pl.ANY)
    near = pl.BlockSpec(memory_space=pltpu.VMEM)
    mo, fg, gw, gk, gg = pl.pallas_call(
        body,
        out_shape=[
            jax.ShapeDtypeStruct((N, D), bf16),
            jax.ShapeDtypeStruct((N, D), bf16),
            jax.ShapeDtypeStruct((RB, 2 * D), bf16),
            jax.ShapeDtypeStruct((K, D), f32),
            jax.ShapeDtypeStruct((D // 128, 128), f32),
        ],
        in_specs=[far, far, far, near, near, near],
        out_specs=[far, far, far, near, near],
        scratch_shapes=[
            V((N, D), bf16), V((N, D), bf16), V((N, N), bf16), V((N, N), bf16), V((N, D), bf16), V((N, D), bf16),
            V((N, 1), f32), V((N, 1), f32), V((N, D), bf16), V((D, N), bf16),
            V((NB, 8, RB, C2), bf16), V((NB, N, C2), bf16), V((N, C2), f32),
            V((LT, L + 2 * R, U, 128), f32), V((LT, L + 2 * R, U, 128), f32), V((N, C), bf16),
            V((K + 1, 8, 128), f32), V((U, 128), jnp.int32), V((N, D), f32),
            V((4, RB, C2), f32), V((2, 4, RB, C2), bf16), V((NB, 4, RB, C2), bf16),
            V((2, 4, 4, RX, C2), bf16), V((NB, 3, 4, RX, C2), bf16),
            V((2, 4, 4, RX, 128), bf16), V((NB, 15, RX, 128), bf16), V((NB, RX, 128), bf16),
            V((NB, 32, C), f32), V((NB, 32, C), f32), V((NB, 4, 8, C), f32), V((NB, 3, 8, C), f32),
            V((NB, 8, C), f32), V((NB, 15, 8, C), f32), V((NB, 4, 8, C), f32),
            V((8, D), f32), V((16, 128), f32), V((16, 128), f32), V((15, 16, 128), f32),
            V((16, 128), f32), V((3, 16, 128), f32), V((16, 128), f32),
            DMA((2,)), DMA((NB,)), DMA((NB, 2)), DMA((NB, 3)), DMA((NB, 3)), DMA((NB, 4)), DMA((NB, 4)),
            DMA((2,)), DMA((NB,)), DMA((2, 3)), DMA((NB, 3)), DMA((2, 15)), DMA((NB, 15)),
            DMA((NB, 15)), DMA((NB, 15)), DMA((NB,)),
            DMA((NB,)), DMA((NB,)), DMA((NB, 3)), DMA((NB, 3)), DMA((NB, 15)), DMA((NB, 15)),
            DMA((NB, 3)), DMA((NB, 3)), DMA((19,)), DMA((19,)),
        ],
        compiler_params=pltpu.CompilerParams(collective_id=0, has_side_effects=True, vmem_limit_bytes=62 << 20),
    )(
        frames.reshape(N, D),
        cotangent.reshape(N, D),
        w_in,
        kernel,
        gain.reshape(D // 128, 128),
        lengths.reshape(16, 128),
    )
    return mo.reshape(U, L, D), fg.reshape(U, L, D), gw.astype(f32), gk, gg.reshape(D)


def solution(mesh):
    rows = P(("dp", "red"), None, None)
    return jax.shard_map(
        local,
        mesh=mesh,
        in_specs=(rows, rows, P("red", None), P(), P(), P()),
        out_specs=(rows, rows, P("red", None), P(), P()),
        check_vma=False,
    )
```

```python
import functools

import jax
import jax.numpy as jnp
from jax import lax
from jax.experimental import pallas as pl
from jax.experimental.pallas import tpu as pltpu
from jax.sharding import PartitionSpec as P

EPSILON = 1e-05
D = 1536
K = 31
R = K // 2
U = 16
L = 48
N = U * L
C = 256
C2 = 2 * C
NB = D // C
LT = C // 128
T = 8
RB = 192
RX = RB // 4
MESH = pl.DeviceIdType.MESH
f32 = jnp.float32
bf16 = jnp.bfloat16


def sigmoid(x):
    return 0.5 * jnp.tanh(0.5 * x) + 0.5


def aligned(i, n):
    return pl.ds(pl.multiple_of(i, n), n)


def body(
    frames, cot, w, kern, gain, lens,
    mo_o, fg_o, gw_o, gk_o, gg_o,
    nat0, nat1, pm, pmt, fr, up, mean, istd, sc, sct, W, gh, h, glu, gcp, mot, kg, len16, gs,
    own, sibs, sibr, s1s, s1r, s2s, s2r, gwp,
    kgl, kgsr, kg1, kg1r, kg2, kg2r, kgo, ggl, ggr, gg2, gg2r, gg3, gg3r, gg4,
    in_sem, mo_sem, wl_sem, wz_s, wz_r, ws_s, ws_r,
    ss_s, ss_r, s1_s, s1_r, s2_s, s2_r, s3_s, s3_r, s3_l,
    ks_s, ks_r, k1_s, k1_r, k2_s, k2_r, k3_s, k3_r, g_s, g_r,
):
    dp, red = lax.axis_index("dp"), lax.axis_index("red")
    x, y = lax.div(dp, 4), lax.rem(dp, 4)
    z, c = lax.div(red, 2), lax.rem(red, 2)

    def turn(a, d):
        return (a + d) & 3

    def at(ax, ay, az, ac):
        return (ax * 4 + ay, az * 2 + ac)

    sib = at(x, y, z, 1 - c)

    def remote(src, dst, ssem, rsem, dev):
        return pltpu.make_async_remote_copy(
            src_ref=src, dst_ref=dst, send_sem=ssem, recv_sem=rsem, device_id=dev, device_id_type=MESH
        )

    def first(b, d):
        p = lax.rem(b, 2)
        return at(turn(x, d * (1 - p)), turn(y, d * p), z, c)

    def plane(b, d, dz):
        p = lax.rem(b, 2)
        return at(turn(x, d * p), turn(y, d * (1 - p)), turn(z, dz), c)

    def place(b):
        p = lax.rem(b, 2)
        return x * (1 - p) + y * p, x * p + y * (1 - p)

    in0 = pltpu.make_async_copy(frames, nat0, in_sem.at[0])
    in0.start()

    def own_w(b, half):
        return pltpu.make_async_copy(
            w.at[:, aligned(half * D + b * C, C)], W.at[b, red, :, pl.ds(half * C, C)], wl_sem.at[b, half]
        )

    for b in range(NB):
        own_w(b, 0).start()
        own_w(b, 1).start()
    in1 = pltpu.make_async_copy(cot, nat1, in_sem.at[1])
    in1.start()

    barrier = pltpu.get_barrier_semaphore()
    offsets = [
        (i, j, k) for i in range(4) for j in range(4) for k in range(4) if (i, j, k) != (0, 0, 0) and i * j * k == 0
    ]
    pl.semaphore_signal(barrier, inc=1, device_id=sib, device_id_type=MESH)
    for i, j, k in offsets:
        pl.semaphore_signal(barrier, inc=1, device_id=at(turn(x, i), turn(y, j), turn(z, k), c), device_id_type=MESH)
    pl.semaphore_wait(barrier, len(offsets) + 1)

    def wz(b, j):
        return remote(W.at[b, red], W.at[b, red], wz_s.at[b, j - 1], wz_r.at[b, j - 1], at(x, y, turn(z, j), c))

    def wsib(b, j):
        held = turn(z, 4 - j) * 2 + c
        return remote(W.at[b, held], W.at[b, held], ws_s.at[b, j], ws_r.at[b, j], sib)

    def send_w(b, _):
        own_w(b, 0).wait()
        own_w(b, 1).wait()
        for j in (1, 3, 2):
            wz(b, j).start()
        wsib(b, 0).start()
        return 0

    def forward_w(b):
        for j in (1, 3, 2):
            wz(b, j).wait_recv()
            wsib(b, j).start()

    def arrived_w(b):
        for j in range(4):
            wsib(b, j).wait_recv()

    def sent_w(b, _):
        for j in (1, 2, 3):
            wz(b, j).wait_send()
        for j in range(4):
            wsib(b, j).wait_send()
        return 0

    lax.fori_loop(0, NB, send_w, 0)

    r0 = lax.broadcasted_iota(jnp.int32, (N, N), 0)
    r1 = lax.broadcasted_iota(jnp.int32, (N, N), 1)
    pm[...] = jnp.where(((r0 & 15) * L + (r0 >> 4)) == r1, 1.0, 0.0).astype(bf16)
    pmt[...] = jnp.where(((r1 & 15) * L + (r1 >> 4)) == r0, 1.0, 0.0).astype(bf16)
    me = dp * 8 + red
    row = lens[pl.ds(lax.div(me, 8), 1), :]
    sub = lax.broadcasted_iota(jnp.int32, (U, 128), 0)
    lane = lax.broadcasted_iota(jnp.int32, (U, 128), 1)
    mine = jnp.where(lane == sub + lax.rem(me, 8) * U, row, 0)
    len16[...] = jnp.broadcast_to(jnp.sum(mine, axis=1, keepdims=True), (U, 128))
    every = jnp.sum(jnp.sum(lens[...], axis=0, keepdims=True), axis=1, keepdims=True)
    root = lax.rsqrt(every.astype(f32))
    glu[...] = jnp.zeros_like(glu)
    gcp[...] = jnp.zeros_like(gcp)
    gg3[...] = jnp.zeros_like(gg3)

    def live(t0, n, lanes):
        t = lax.broadcasted_iota(jnp.int32, (n, U, lanes), 0) + t0
        return t < len16[:, :lanes][None]

    in0.wait()
    PR = 256

    def perm_frames(i, _):
        rows = aligned(i * PR, PR)
        fr[rows, :] = jnp.dot(pm[rows, :], nat0[...], preferred_element_type=f32).astype(bf16)
        return 0

    lax.fori_loop(0, N // PR, perm_frames, 0)

    gain_row = jnp.concatenate([gain[q : q + 1, :] for q in range(D // 128)], axis=1)

    def norm(i, _):
        NR = 128
        rows = aligned(i * NR, NR)
        v = fr[rows, :].astype(f32)
        m = jnp.mean(v, axis=-1, keepdims=True)
        cen = v - m
        s = lax.rsqrt(jnp.mean(cen * cen, axis=-1, keepdims=True) + EPSILON)
        mean[rows, :] = m
        istd[rows, :] = s
        scaled = cen * s * gain_row
        sc[rows, :] = scaled.astype(bf16)
        turned = scaled.T.astype(bf16)
        for q in range(8):
            other = lax.rem(c + q % 2, 2)
            dst = other * (4 * RB) + (q // 2) * RB
            sct[aligned_rows(dst, RB), rows] = turned[q * RB : (q + 1) * RB, :]
        return 0

    def aligned_rows(i, n):
        return pl.ds(pl.multiple_of(i, 64), n)

    lax.fori_loop(0, N // 128, norm, 0)
    in1.wait()

    def perm_cot(i, _):
        rows = aligned(i * PR, PR)
        v = jnp.dot(pm[rows, :], nat1[...], preferred_element_type=f32).reshape(PR // U, U, D)
        up[rows, :] = jnp.where(live(i * (PR // U), PR // U, 1), v, 0.0).reshape(PR, D).astype(bf16)
        return 0

    lax.fori_loop(0, N // PR, perm_cot, 0)

    def sib_send(b):
        return remote(sibs.at[lax.rem(b, 2)], sibr.at[b], ss_s.at[lax.rem(b, 2)], ss_r.at[b], sib)

    def ksib(b):
        return remote(kgl.at[lax.div(b, 3)], kgsr.at[lax.div(b, 3)], ks_s.at[lax.div(b, 3)], ks_r.at[lax.div(b, 3)], sib)

    def s1(b, j):
        p = lax.rem(b, 2)
        f, _ = place(b)
        return remote(s1s.at[p, turn(f, j)], s1r.at[b, j - 1], s1_s.at[p, j - 1], s1_r.at[b, j - 1], first(b, j))

    def k1(b, j):
        f, _ = place(b)
        g = lax.div(b, 3)
        return remote(kg1.at[g, turn(f, j)], kg1r.at[g, j - 1], k1_s.at[g, j - 1], k1_r.at[g, j - 1], first(b, j))

    def s2(b, i):
        p = lax.rem(b, 2)
        _, s = place(b)
        d, dz = i // 4, i % 4
        return remote(
            s2s.at[p, turn(s, d), turn(z, dz)], s2r.at[b, i - 1], s2_s.at[p, i - 1], s2_r.at[b, i - 1], plane(b, d, dz)
        )

    def k2(b, i):
        d, dz = i // 4, i % 4
        g = lax.div(b, 3)
        return remote(kg2.at[g], kg2r.at[g, i - 1], k2_s.at[g, i - 1], k2_r.at[g, i - 1], plane(b, d, dz))

    def piece(b):
        f, s = place(b)
        return gw_o.at[aligned(f * RX, RX), aligned(lax.div(s, 2) * D + b * C + lax.rem(s, 2) * 128, 128)]

    def s3(b, i):
        dev = at(turn(x, i // 4), turn(y, i % 4), z, c)
        return remote(gwp.at[b], piece(b), s3_s.at[b, i - 1], s3_r.at[b, i - 1], dev)

    def s3_own(b):
        return pltpu.make_async_copy(gwp.at[b], piece(b), s3_l.at[b])

    def k3(b, j):
        f, _ = place(b)
        g = lax.div(b, 3)
        return remote(kgo.at[g, f], kgo.at[g, f], k3_s.at[g, j - 1], k3_r.at[g, j - 1], first(b, j))

    def loop15(fn):
        for i in range(1, 16):
            fn(i)

    def stage1(b):
        p = lax.rem(b, 2)
        sib_send(b).wait_recv()

        @pl.when(b >= 2)
        def _():
            for j in (1, 2, 3):
                s1(b - 2, j).wait_send()

        def add(q, _):
            v = own[q] + sibr[b, q].astype(f32)
            for f in range(4):
                s1s[p, f, q] = v[f * RX : (f + 1) * RX].astype(bf16)
            return 0

        lax.fori_loop(0, 4, add, 0)
        for j in (1, 3, 2):
            s1(b, j).start()

        @pl.when(lax.rem(b, 3) == 2)
        def _():
            g = lax.div(b, 3)
            ksib(b).wait_recv()
            t = kgl[g] + kgsr[g]
            for f in range(4):
                kg1[g, f] = t[f * 8 : (f + 1) * 8]
            for j in (1, 3, 2):
                k1(b, j).start()

    def stage2(b):
        p = lax.rem(b, 2)
        f, _ = place(b)
        for j in (1, 2, 3):
            s1(b, j).wait_recv()

        @pl.when(b >= 2)
        def _():
            loop15(lambda i: s2(b - 2, i).wait_send())

        def add(q, _):
            v = s1s[p, f, q].astype(f32)
            for j in range(3):
                v = v + s1r[b, j, q].astype(f32)
            for s in range(4):
                s2s[p, s, q] = v[:, s * 128 : (s + 1) * 128].astype(bf16)
            return 0

        lax.fori_loop(0, 4, add, 0)
        loop15(lambda i: s2(b, i).start())

        @pl.when(lax.rem(b, 3) == 2)
        def _():
            g = lax.div(b, 3)
            for j in (1, 2, 3):
                k1(b, j).wait_recv()
            kg2[g] = kg1[g, f] + kg1r[g, 0] + kg1r[g, 1] + kg1r[g, 2]
            loop15(lambda i: k2(b, i).start())

    def stage3(b):
        p = lax.rem(b, 2)
        f, s = place(b)
        loop15(lambda i: s2(b, i).wait_recv())
        v = s2s[p, s, z].astype(f32)
        for i in range(15):
            v = v + s2r[b, i].astype(f32)
        gwp[b] = (v * root).astype(bf16)
        loop15(lambda i: s3(b, i).start())
        s3_own(b).start()

        @pl.when(lax.rem(b, 3) == 2)
        def _():
            g = lax.div(b, 3)
            loop15(lambda i: k2(b, i).wait_recv())
            t = kg2[g]
            for i in range(15):
                t = t + kg2r[g, i]
            kgo[g, f] = t * root
            for j in (1, 2, 3):
                k3(b, j).start()

    def put_taps(b, lt):
        kgl[lax.div(b, 3), :, aligned(lax.rem(b, 3) * C + lt * 128, 128)] = jnp.sum(kg[...], axis=1)

    def trimmed(step, at_start, at_end):
        step(0, at_start)

        def inner(i, _):
            step(i, range(K))
            return 0

        lax.fori_loop(1, L // T - 1, inner, 0)
        step(L // T - 1, at_end)

    def block(b, _):
        forward_first = b == 0

        @pl.when(forward_first)
        def _():
            forward_w(b)

        arrived_w(b)

        h[...] = jnp.dot(sc[...], W[b].reshape(D, C2), preferred_element_type=f32)

        @pl.when(b >= 1)
        def _():
            stage1(b - 1)

        for lt in range(LT):
            vl = slice(lt * 128, (lt + 1) * 128)
            gl = slice(C + lt * 128, C + (lt + 1) * 128)
            cl = aligned(b * C + lt * 128, 128)

            def gate(i, _):
                rows = aligned(i * (T * U), T * U)
                s = sigmoid(h[rows, gl])
                h[rows, gl] = s
                out = jnp.where(live(i * T, T, 128), (h[rows, vl] * s).reshape(T, U, 128), 0.0)
                glu[lt, pl.ds(i * T + R, T)] = out
                return 0

            lax.fori_loop(0, L // T, gate, 0)
            kg[...] = jnp.zeros_like(kg)

            def forward(i, taps):
                t0 = i * T
                rows = aligned(i * (T * U), T * U)
                acc = jnp.zeros((T, U, 128), f32)
                for k in taps:
                    acc = acc + kern[k : k + 1, cl][None] * glu[lt, pl.ds(t0 + k, T)]
                s = sigmoid(acc)
                swish = acc * s
                out = jnp.where(live(t0, T, 128), fr[rows, cl].astype(f32).reshape(T, U, 128) + swish, 0.0)
                mot[rows, vl] = out.reshape(T * U, 128).astype(bf16)
                gc = up[rows, cl].astype(f32).reshape(T, U, 128) * (s + swish * (1.0 - s))
                gcp[lt, pl.ds(t0 + R, T)] = gc
                for k in taps:
                    p = jnp.sum(gc * glu[lt, pl.ds(t0 + k, T)], axis=0)
                    kg[k] += p[0:8] + p[8:16]

            trimmed(forward, range(T, K), range(K - T))
            put_taps(b, lt)

            def backward(i, taps):
                t0 = i * T
                rows = aligned(i * (T * U), T * U)
                acc = jnp.zeros((T, U, 128), f32)
                for k in taps:
                    acc = acc + kern[k : k + 1, cl][None] * gcp[lt, pl.ds(t0 + (K - 1) - k, T)]
                dg = jnp.where(live(t0, T, 128), acc, 0.0)
                s = h[rows, gl].reshape(T, U, 128)
                gh[b, rows, vl] = (dg * s).reshape(T * U, 128).astype(bf16)
                gate_part = dg * glu[lt, pl.ds(t0 + R, T)] * (1.0 - s)
                gh[b, rows, gl] = gate_part.reshape(T * U, 128).astype(bf16)

            trimmed(backward, range(K - T), range(T, K))

        @pl.when(b + 1 < NB)
        def _():
            forward_w(b + 1)

        @pl.when(b >= 2)
        def _():
            sib_send(b - 2).wait_send()

        g = jnp.dot(sct[4 * RB :, :], gh[b], preferred_element_type=f32).astype(bf16)
        sibs[lax.rem(b, 2)] = g.reshape(4, RB, C2)
        sib_send(b).start()

        @pl.when(lax.rem(b, 3) == 2)
        def _():
            ksib(b).start()

        own[...] = jnp.dot(sct[: 4 * RB, :], gh[b], preferred_element_type=f32).reshape(4, RB, C2)

        @pl.when(b >= 3)
        def _():
            stage3(b - 3)

        @pl.when(b >= 2)
        def _():
            stage2(b - 2)

        cols = aligned(b * C, C)

        nat0[:, cols] = jnp.dot(pmt[...], mot[...], preferred_element_type=f32).astype(bf16)
        mo_copy(b).start()
        return 0

    def mo_copy(b):
        cols = aligned(b * C, C)
        return pltpu.make_async_copy(nat0.at[:, cols], mo_o.at[:, cols], mo_sem.at[b])

    lax.fori_loop(0, NB, block, 0)

    stage1(NB - 1)
    stage2(NB - 2)
    ggl[...] = jnp.zeros_like(ggl)

    def g1():
        return remote(gg3, ggr, g_s.at[18], g_r.at[18], sib)

    def g2(i):
        return remote(gg2, gg2r.at[i - 1], g_s.at[i - 1], g_r.at[i - 1], plane(0, i // 4, i % 4))

    def g3(j):
        return remote(gg4, gg3r.at[j - 1], g_s.at[14 + j], g_r.at[14 + j], first(0, j))

    def acc(b, _):
        p = lax.dot_general(gh[b], W[b].reshape(D, C2), (((1,), (1,)), ((), ())), preferred_element_type=f32)

        @pl.when(b == 0)
        def _():
            gs[...] = p

        @pl.when(b > 0)
        def _():
            gs[...] += p

        @pl.when(b == 1)
        def _():
            stage3(NB - 3)

        @pl.when(b == 4)
        def _():
            stage3(NB - 2)

        return 0

    lax.fori_loop(0, NB, acc, 0)
    NR = 64

    def normed(r):
        return (fr[r, :].astype(f32) - mean[r, :]) * istd[r, :]

    def gain_part(j, _):
        r = aligned(j * NR, NR)
        ggl[...] += jnp.sum((gs[r, :] * normed(r)).reshape(NR // 8, 8, D), axis=0)
        return 0

    lax.fori_loop(0, N // NR, gain_part, 0)
    total = jnp.sum(ggl[...], axis=0, keepdims=True)
    for q in range(D // 128):
        gg3[q : q + 1, :] = total[:, q * 128 : (q + 1) * 128]
    g1().start()

    def ln(j, _):
        @pl.when(j == 3)
        def _():
            g1().wait_recv()
            gg2[...] = gg3[...] + ggr[...]
            loop15(lambda i: g2(i).start())

        @pl.when(j == 5)
        def _():
            stage2(NB - 1)

        r = aligned(j * NR, NR)
        s = istd[r, :]
        nm = normed(r)
        g = gs[r, :] * gain_row
        m1 = jnp.mean(g, axis=-1, keepdims=True)
        m2 = jnp.mean(g * nm, axis=-1, keepdims=True)
        o = up[r, :].astype(f32) + s * (g - m1 - nm * m2)
        lv = live(j * (NR // U), NR // U, 1)
        nat1[r, :] = jnp.where(lv, o.reshape(NR // U, U, D), 0.0).reshape(NR, D).astype(bf16)
        return 0

    lax.fori_loop(0, N // NR, ln, 0)

    def mo_done(b, _):
        mo_copy(b).wait()
        return 0

    lax.fori_loop(0, NB, mo_done, 0)
    nat0[...] = jnp.dot(pmt[...], nat1[...], preferred_element_type=f32).astype(bf16)
    fg_copy = pltpu.make_async_copy(nat0, fg_o, in_sem.at[0])
    fg_copy.start()
    loop15(lambda i: g2(i).wait_recv())
    t = gg2[...]
    for i in range(15):
        t = t + gg2r[i]
    gg4[...] = t
    for j in (1, 2, 3):
        g3(j).start()
    stage3(NB - 1)

    def done(b, _):
        loop15(lambda i: s3(b, i).wait())
        s3_own(b).wait()
        return 0

    for b in (2, 5):
        for j in (1, 2, 3):
            k3(b, j).wait()
            k1(b, j).wait_send()
        ksib(b).wait_send()
        loop15(lambda i: k2(b, i).wait_send())
        g = b // 3
        gk_o[:, g * 3 * C : (g + 1) * 3 * C] = kgo[g].reshape(32, 3 * C)[0:K]

    lax.fori_loop(0, NB, done, 0)
    lax.fori_loop(0, NB, sent_w, 0)
    for b in (NB - 2, NB - 1):
        sib_send(b).wait_send()
        for j in (1, 2, 3):
            s1(b, j).wait_send()
        loop15(lambda i: s2(b, i).wait_send())
    g1().wait_send()
    loop15(lambda i: g2(i).wait_send())
    for j in (1, 2, 3):
        g3(j).wait()
    gg_o[...] = ((gg4[...] + gg3r[0] + gg3r[1] + gg3r[2]) * root)[0 : D // 128]
    fg_copy.wait()


def local(frames, cotangent, w_in, kernel, gain, lengths):
    V, DMA = pltpu.VMEM, pltpu.SemaphoreType.DMA
    far = pl.BlockSpec(memory_space=pl.ANY)
    near = pl.BlockSpec(memory_space=pltpu.VMEM)
    mo, fg, gw, gk, gg = pl.pallas_call(
        body,
        out_shape=[
            jax.ShapeDtypeStruct((N, D), bf16),
            jax.ShapeDtypeStruct((N, D), bf16),
            jax.ShapeDtypeStruct((RB, 2 * D), bf16),
            jax.ShapeDtypeStruct((K, D), f32),
            jax.ShapeDtypeStruct((D // 128, 128), f32),
        ],
        in_specs=[far, far, far, near, near, near],
        out_specs=[far, far, far, near, near],
        scratch_shapes=[
            V((N, D), bf16), V((N, D), bf16), V((N, N), bf16), V((N, N), bf16), V((N, D), bf16), V((N, D), bf16),
            V((N, 1), f32), V((N, 1), f32), V((N, D), bf16), V((D, N), bf16),
            V((NB, 8, RB, C2), bf16), V((NB, N, C2), bf16), V((N, C2), f32),
            V((LT, L + 2 * R, U, 128), f32), V((LT, L + 2 * R, U, 128), f32), V((N, C), bf16),
            V((K + 1, 8, 128), f32), V((U, 128), jnp.int32), V((N, D), f32),
            V((4, RB, C2), f32), V((2, 4, RB, C2), bf16), V((NB, 4, RB, C2), bf16),
            V((2, 4, 4, RX, C2), bf16), V((NB, 3, 4, RX, C2), bf16),
            V((2, 4, 4, RX, 128), bf16), V((NB, 15, RX, 128), bf16), V((NB, RX, 128), bf16),
            V((2, 32, 3 * C), f32), V((2, 32, 3 * C), f32), V((2, 4, 8, 3 * C), f32), V((2, 3, 8, 3 * C), f32),
            V((2, 8, 3 * C), f32), V((2, 15, 8, 3 * C), f32), V((2, 4, 8, 3 * C), f32),
            V((8, D), f32), V((16, 128), f32), V((16, 128), f32), V((15, 16, 128), f32),
            V((16, 128), f32), V((3, 16, 128), f32), V((16, 128), f32),
            DMA((2,)), DMA((NB,)), DMA((NB, 2)), DMA((NB, 3)), DMA((NB, 3)), DMA((NB, 4)), DMA((NB, 4)),
            DMA((2,)), DMA((NB,)), DMA((2, 3)), DMA((NB, 3)), DMA((2, 15)), DMA((NB, 15)),
            DMA((NB, 15)), DMA((NB, 15)), DMA((NB,)),
            DMA((2,)), DMA((2,)), DMA((2, 3)), DMA((2, 3)), DMA((2, 15)), DMA((2, 15)),
            DMA((2, 3)), DMA((2, 3)), DMA((19,)), DMA((19,)),
        ],
        compiler_params=pltpu.CompilerParams(collective_id=0, has_side_effects=True, vmem_limit_bytes=62 << 20),
    )(
        frames.reshape(N, D),
        cotangent.reshape(N, D),
        w_in,
        kernel,
        gain.reshape(D // 128, 128),
        lengths.reshape(16, 128),
    )
    return mo.reshape(U, L, D), fg.reshape(U, L, D), gw.astype(f32), gk, gg.reshape(D)


def solution(mesh):
    rows = P(("dp", "red"), None, None)
    return jax.shard_map(
        local,
        mesh=mesh,
        in_specs=(rows, rows, P("red", None), P(), P(), P()),
        out_specs=(rows, rows, P("red", None), P(), P()),
        check_vma=False,
    )
```

```python
import functools

import jax
import jax.numpy as jnp
from jax import lax
from jax.experimental import pallas as pl
from jax.experimental.pallas import tpu as pltpu
from jax.sharding import PartitionSpec as P

EPSILON = 1e-05
D = 1536
K = 31
R = K // 2
U = 16
L = 48
N = U * L
C = 256
C2 = 2 * C
NB = D // C
LT = C // 128
T = 8
RB = 192
RX = RB // 4
MESH = pl.DeviceIdType.MESH
f32 = jnp.float32
bf16 = jnp.bfloat16


def sigmoid(x):
    return 0.5 * jnp.tanh(0.5 * x) + 0.5


def aligned(i, n):
    return pl.ds(pl.multiple_of(i, n), n)


def body(
    frames, cot, w, kern, gain, lens,
    mo_o, fg_o, gw_o, gk_o, gg_o,
    nat0, nat1, pm, pmt, fr, up, mean, istd, sc, sct, W, gh, h, glu, gcp, kg, len16, gs,
    own, sibs, sibr, s1s, s1r, s2s, s2r, gwp,
    kgl, kgsr, kg1, kg1r, kg2, kg2r, kgo, ggl, ggr, gg2, gg2r, gg3, gg3r, gg4,
    in_sem, mo_sem, wl_sem, wz_s, wz_r, ws_s, ws_r,
    ss_s, ss_r, s1_s, s1_r, s2_s, s2_r, s3_s, s3_r, s3_l,
    ks_s, ks_r, k1_s, k1_r, k2_s, k2_r, k3_s, k3_r, g_s, g_r,
):
    dp, red = lax.axis_index("dp"), lax.axis_index("red")
    x, y = lax.div(dp, 4), lax.rem(dp, 4)
    z, c = lax.div(red, 2), lax.rem(red, 2)

    def turn(a, d):
        return (a + d) & 3

    def at(ax, ay, az, ac):
        return (ax * 4 + ay, az * 2 + ac)

    sib = at(x, y, z, 1 - c)

    def remote(src, dst, ssem, rsem, dev):
        return pltpu.make_async_remote_copy(
            src_ref=src, dst_ref=dst, send_sem=ssem, recv_sem=rsem, device_id=dev, device_id_type=MESH
        )

    def first(b, d):
        p = lax.rem(b, 2)
        return at(turn(x, d * (1 - p)), turn(y, d * p), z, c)

    def plane(b, d, dz):
        p = lax.rem(b, 2)
        return at(turn(x, d * p), turn(y, d * (1 - p)), turn(z, dz), c)

    def place(b):
        p = lax.rem(b, 2)
        return x * (1 - p) + y * p, x * p + y * (1 - p)

    in0 = pltpu.make_async_copy(frames, nat0, in_sem.at[0])
    in0.start()

    def own_w(b, half):
        return pltpu.make_async_copy(
            w.at[:, aligned(half * D + b * C, C)], W.at[b, red, :, pl.ds(half * C, C)], wl_sem.at[b, half]
        )

    for b in range(NB):
        own_w(b, 0).start()
        own_w(b, 1).start()
    in1 = pltpu.make_async_copy(cot, nat1, in_sem.at[1])
    in1.start()

    barrier = pltpu.get_barrier_semaphore()
    offsets = [
        (i, j, k) for i in range(4) for j in range(4) for k in range(4) if (i, j, k) != (0, 0, 0) and i * j * k == 0
    ]
    pl.semaphore_signal(barrier, inc=1, device_id=sib, device_id_type=MESH)
    for i, j, k in offsets:
        pl.semaphore_signal(barrier, inc=1, device_id=at(turn(x, i), turn(y, j), turn(z, k), c), device_id_type=MESH)
    pl.semaphore_wait(barrier, len(offsets) + 1)

    def wz(b, j):
        return remote(W.at[b, red], W.at[b, red], wz_s.at[b, j - 1], wz_r.at[b, j - 1], at(x, y, turn(z, j), c))

    def wsib(b, j):
        held = turn(z, 4 - j) * 2 + c
        return remote(W.at[b, held], W.at[b, held], ws_s.at[b, j], ws_r.at[b, j], sib)

    def send_w(b, _):
        own_w(b, 0).wait()
        own_w(b, 1).wait()
        for j in (1, 3, 2):
            wz(b, j).start()
        wsib(b, 0).start()
        return 0

    def forward_w(b):
        for j in (1, 3, 2):
            wz(b, j).wait_recv()
            wsib(b, j).start()

    def arrived_w(b):
        for j in range(4):
            wsib(b, j).wait_recv()

    def sent_w(b, _):
        for j in (1, 2, 3):
            wz(b, j).wait_send()
        for j in range(4):
            wsib(b, j).wait_send()
        return 0

    lax.fori_loop(0, NB, send_w, 0)

    r0 = lax.broadcasted_iota(jnp.int32, (N, N), 0)
    r1 = lax.broadcasted_iota(jnp.int32, (N, N), 1)
    pm[...] = jnp.where(((r0 & 15) * L + (r0 >> 4)) == r1, 1.0, 0.0).astype(bf16)
    pmt[...] = jnp.where(((r1 & 15) * L + (r1 >> 4)) == r0, 1.0, 0.0).astype(bf16)
    me = dp * 8 + red
    row = lens[pl.ds(lax.div(me, 8), 1), :]
    sub = lax.broadcasted_iota(jnp.int32, (U, 128), 0)
    lane = lax.broadcasted_iota(jnp.int32, (U, 128), 1)
    mine = jnp.where(lane == sub + lax.rem(me, 8) * U, row, 0)
    len16[...] = jnp.broadcast_to(jnp.sum(mine, axis=1, keepdims=True), (U, 128))
    every = jnp.sum(jnp.sum(lens[...], axis=0, keepdims=True), axis=1, keepdims=True)
    root = lax.rsqrt(every.astype(f32))
    glu[...] = jnp.zeros_like(glu)
    gcp[...] = jnp.zeros_like(gcp)
    gg3[...] = jnp.zeros_like(gg3)

    def live(t0, n, lanes):
        t = lax.broadcasted_iota(jnp.int32, (n, U, lanes), 0) + t0
        return t < len16[:, :lanes][None]

    in0.wait()
    PR = 256

    def perm_frames(i, _):
        rows = aligned(i * PR, PR)
        fr[rows, :] = jnp.dot(pm[rows, :], nat0[...], preferred_element_type=f32).astype(bf16)
        return 0

    lax.fori_loop(0, N // PR, perm_frames, 0)

    gain_row = jnp.concatenate([gain[q : q + 1, :] for q in range(D // 128)], axis=1)

    def norm(i, _):
        NR = 128
        rows = aligned(i * NR, NR)
        v = fr[rows, :].astype(f32)
        m = jnp.mean(v, axis=-1, keepdims=True)
        cen = v - m
        s = lax.rsqrt(jnp.mean(cen * cen, axis=-1, keepdims=True) + EPSILON)
        mean[rows, :] = m
        istd[rows, :] = s
        scaled = cen * s * gain_row
        sc[rows, :] = scaled.astype(bf16)
        turned = scaled.T.astype(bf16)
        for q in range(8):
            other = lax.rem(c + q % 2, 2)
            dst = other * (4 * RB) + (q // 2) * RB
            sct[aligned_rows(dst, RB), rows] = turned[q * RB : (q + 1) * RB, :]
        return 0

    def aligned_rows(i, n):
        return pl.ds(pl.multiple_of(i, 64), n)

    lax.fori_loop(0, N // 128, norm, 0)
    in1.wait()

    def perm_cot(i, _):
        rows = aligned(i * PR, PR)
        v = jnp.dot(pm[rows, :], nat1[...], preferred_element_type=f32).reshape(PR // U, U, D)
        up[rows, :] = jnp.where(live(i * (PR // U), PR // U, 1), v, 0.0).reshape(PR, D).astype(bf16)
        return 0

    lax.fori_loop(0, N // PR, perm_cot, 0)

    def sib_send(b):
        return remote(sibs.at[lax.rem(b, 2)], sibr.at[b], ss_s.at[lax.rem(b, 2)], ss_r.at[b], sib)

    def ksib(b):
        return remote(kgl.at[lax.div(b, 3)], kgsr.at[lax.div(b, 3)], ks_s.at[lax.div(b, 3)], ks_r.at[lax.div(b, 3)], sib)

    def s1(b, j):
        p = lax.rem(b, 2)
        f, _ = place(b)
        return remote(s1s.at[p, turn(f, j)], s1r.at[b, j - 1], s1_s.at[p, j - 1], s1_r.at[b, j - 1], first(b, j))

    def k1(b, j):
        f, _ = place(b)
        g = lax.div(b, 3)
        return remote(kg1.at[g, turn(f, j)], kg1r.at[g, j - 1], k1_s.at[g, j - 1], k1_r.at[g, j - 1], first(b, j))

    def s2(b, i):
        p = lax.rem(b, 2)
        _, s = place(b)
        d, dz = i // 4, i % 4
        return remote(
            s2s.at[p, turn(s, d), turn(z, dz)], s2r.at[b, i - 1], s2_s.at[p, i - 1], s2_r.at[b, i - 1], plane(b, d, dz)
        )

    def k2(b, i):
        d, dz = i // 4, i % 4
        g = lax.div(b, 3)
        return remote(kg2.at[g], kg2r.at[g, i - 1], k2_s.at[g, i - 1], k2_r.at[g, i - 1], plane(b, d, dz))

    def piece(b):
        f, s = place(b)
        return gw_o.at[aligned(f * RX, RX), aligned(lax.div(s, 2) * D + b * C + lax.rem(s, 2) * 128, 128)]

    def s3(b, i):
        dev = at(turn(x, i // 4), turn(y, i % 4), z, c)
        return remote(gwp.at[b], piece(b), s3_s.at[b, i - 1], s3_r.at[b, i - 1], dev)

    def s3_own(b):
        return pltpu.make_async_copy(gwp.at[b], piece(b), s3_l.at[b])

    def k3(b, j):
        f, _ = place(b)
        g = lax.div(b, 3)
        return remote(kgo.at[g, f], kgo.at[g, f], k3_s.at[g, j - 1], k3_r.at[g, j - 1], first(b, j))

    def loop15(fn):
        for i in range(1, 16):
            fn(i)

    def stage1(b):
        p = lax.rem(b, 2)
        sib_send(b).wait_recv()

        @pl.when(b >= 2)
        def _():
            for j in (1, 2, 3):
                s1(b - 2, j).wait_send()

        def add(q, _):
            v = own[q] + sibr[b, q].astype(f32)
            for f in range(4):
                s1s[p, f, q] = v[f * RX : (f + 1) * RX].astype(bf16)
            return 0

        lax.fori_loop(0, 4, add, 0)
        for j in (1, 3, 2):
            s1(b, j).start()

        @pl.when(lax.rem(b, 3) == 2)
        def _():
            g = lax.div(b, 3)
            ksib(b).wait_recv()
            t = kgl[g] + kgsr[g]
            for f in range(4):
                kg1[g, f] = t[f * 8 : (f + 1) * 8]
            for j in (1, 3, 2):
                k1(b, j).start()

    def stage2(b):
        p = lax.rem(b, 2)
        f, _ = place(b)
        for j in (1, 2, 3):
            s1(b, j).wait_recv()

        @pl.when(b >= 2)
        def _():
            loop15(lambda i: s2(b - 2, i).wait_send())

        def add(q, _):
            v = s1s[p, f, q].astype(f32)
            for j in range(3):
                v = v + s1r[b, j, q].astype(f32)
            for s in range(4):
                s2s[p, s, q] = v[:, s * 128 : (s + 1) * 128].astype(bf16)
            return 0

        lax.fori_loop(0, 4, add, 0)
        loop15(lambda i: s2(b, i).start())

        @pl.when(lax.rem(b, 3) == 2)
        def _():
            g = lax.div(b, 3)
            for j in (1, 2, 3):
                k1(b, j).wait_recv()
            kg2[g] = kg1[g, f] + kg1r[g, 0] + kg1r[g, 1] + kg1r[g, 2]
            loop15(lambda i: k2(b, i).start())

    def stage3(b):
        p = lax.rem(b, 2)
        f, s = place(b)
        loop15(lambda i: s2(b, i).wait_recv())
        v = s2s[p, s, z].astype(f32)
        for i in range(15):
            v = v + s2r[b, i].astype(f32)
        gwp[b] = (v * root).astype(bf16)
        loop15(lambda i: s3(b, i).start())
        s3_own(b).start()

        @pl.when(lax.rem(b, 3) == 2)
        def _():
            g = lax.div(b, 3)
            loop15(lambda i: k2(b, i).wait_recv())
            t = kg2[g]
            for i in range(15):
                t = t + kg2r[g, i]
            kgo[g, f] = t * root
            for j in (1, 2, 3):
                k3(b, j).start()

    def put_taps(b, lt):
        kgl[lax.div(b, 3), :, aligned(lax.rem(b, 3) * C + lt * 128, 128)] = jnp.sum(kg[...], axis=1)

    def trimmed(step, at_start, at_end):
        step(0, at_start)

        def inner(i, _):
            step(i, range(K))
            return 0

        lax.fori_loop(1, L // T - 1, inner, 0)
        step(L // T - 1, at_end)

    def block(b, _):
        forward_first = b == 0

        @pl.when(forward_first)
        def _():
            forward_w(b)

        arrived_w(b)

        h[...] = jnp.dot(sc[...], W[b].reshape(D, C2), preferred_element_type=f32)

        @pl.when(b >= 4)
        def _():
            stage3(b - 4)

        @pl.when(b >= 3)
        def _():
            stage2(b - 3)

        @pl.when(b >= 1)
        def _():
            stage1(b - 1)

        for lt in range(LT):
            vl = slice(lt * 128, (lt + 1) * 128)
            gl = slice(C + lt * 128, C + (lt + 1) * 128)
            cl = aligned(b * C + lt * 128, 128)

            def gate(i, _):
                rows = aligned(i * (T * U), T * U)
                s = sigmoid(h[rows, gl])
                h[rows, gl] = s
                out = jnp.where(live(i * T, T, 128), (h[rows, vl] * s).reshape(T, U, 128), 0.0)
                glu[lt, pl.ds(i * T + R, T)] = out
                return 0

            lax.fori_loop(0, L // T, gate, 0)
            kg[...] = jnp.zeros_like(kg)

            def forward(i, taps):
                t0 = i * T
                rows = aligned(i * (T * U), T * U)
                acc = jnp.zeros((T, U, 128), f32)
                for k in taps:
                    acc = acc + kern[k : k + 1, cl][None] * glu[lt, pl.ds(t0 + k, T)]
                s = sigmoid(acc)
                swish = acc * s
                out = jnp.where(live(t0, T, 128), fr[rows, cl].astype(f32).reshape(T, U, 128) + swish, 0.0)
                nat0[rows, cl] = out.reshape(T * U, 128).astype(bf16)
                gc = up[rows, cl].astype(f32).reshape(T, U, 128) * (s + swish * (1.0 - s))
                gcp[lt, pl.ds(t0 + R, T)] = gc
                for k in taps:
                    p = jnp.sum(gc * glu[lt, pl.ds(t0 + k, T)], axis=0)
                    kg[k] += p[0:8] + p[8:16]

            trimmed(forward, range(T, K), range(K - T))
            put_taps(b, lt)

            def backward(i, taps):
                t0 = i * T
                rows = aligned(i * (T * U), T * U)
                acc = jnp.zeros((T, U, 128), f32)
                for k in taps:
                    acc = acc + kern[k : k + 1, cl][None] * gcp[lt, pl.ds(t0 + (K - 1) - k, T)]
                dg = jnp.where(live(t0, T, 128), acc, 0.0)
                s = h[rows, gl].reshape(T, U, 128)
                gh[b, rows, vl] = (dg * s).reshape(T * U, 128).astype(bf16)
                gate_part = dg * glu[lt, pl.ds(t0 + R, T)] * (1.0 - s)
                gh[b, rows, gl] = gate_part.reshape(T * U, 128).astype(bf16)

            trimmed(backward, range(K - T), range(T, K))

        @pl.when(b + 1 < NB)
        def _():
            forward_w(b + 1)

        @pl.when(b >= 2)
        def _():
            sib_send(b - 2).wait_send()

        g = jnp.dot(sct[4 * RB :, :], gh[b], preferred_element_type=f32).astype(bf16)
        sibs[lax.rem(b, 2)] = g.reshape(4, RB, C2)
        sib_send(b).start()

        @pl.when(lax.rem(b, 3) == 2)
        def _():
            ksib(b).start()

        own[...] = jnp.dot(sct[: 4 * RB, :], gh[b], preferred_element_type=f32).reshape(4, RB, C2)
        return 0

    lax.fori_loop(0, NB, block, 0)

    stage2(NB - 3)
    stage1(NB - 1)
    sc[...] = jnp.dot(pmt[...], nat0[...], preferred_element_type=f32).astype(bf16)
    mo_copy = pltpu.make_async_copy(sc, mo_o, mo_sem.at[0])
    mo_copy.start()
    stage3(NB - 4)
    stage2(NB - 2)
    ggl[...] = jnp.zeros_like(ggl)

    def g1():
        return remote(gg3, ggr, g_s.at[18], g_r.at[18], sib)

    def g2(i):
        return remote(gg2, gg2r.at[i - 1], g_s.at[i - 1], g_r.at[i - 1], plane(0, i // 4, i % 4))

    def g3(j):
        return remote(gg4, gg3r.at[j - 1], g_s.at[14 + j], g_r.at[14 + j], first(0, j))

    def acc(b, _):
        p = lax.dot_general(gh[b], W[b].reshape(D, C2), (((1,), (1,)), ((), ())), preferred_element_type=f32)

        @pl.when(b == 0)
        def _():
            gs[...] = p

        @pl.when(b > 0)
        def _():
            gs[...] += p

        @pl.when(b == 1)
        def _():
            stage3(NB - 3)

        @pl.when(b == 4)
        def _():
            stage3(NB - 2)

        return 0

    lax.fori_loop(0, NB, acc, 0)
    NR = 64

    def normed(r):
        return (fr[r, :].astype(f32) - mean[r, :]) * istd[r, :]

    def gain_part(j, _):
        r = aligned(j * NR, NR)
        ggl[...] += jnp.sum((gs[r, :] * normed(r)).reshape(NR // 8, 8, D), axis=0)
        return 0

    lax.fori_loop(0, N // NR, gain_part, 0)
    total = jnp.sum(ggl[...], axis=0, keepdims=True)
    for q in range(D // 128):
        gg3[q : q + 1, :] = total[:, q * 128 : (q + 1) * 128]
    g1().start()

    def ln(j, _):
        @pl.when(j == 3)
        def _():
            g1().wait_recv()
            gg2[...] = gg3[...] + ggr[...]
            loop15(lambda i: g2(i).start())

        @pl.when(j == 0)
        def _():
            stage2(NB - 1)

        r = aligned(j * NR, NR)
        s = istd[r, :]
        nm = normed(r)
        g = gs[r, :] * gain_row
        m1 = jnp.mean(g, axis=-1, keepdims=True)
        m2 = jnp.mean(g * nm, axis=-1, keepdims=True)
        o = up[r, :].astype(f32) + s * (g - m1 - nm * m2)
        lv = live(j * (NR // U), NR // U, 1)
        nat1[r, :] = jnp.where(lv, o.reshape(NR // U, U, D), 0.0).reshape(NR, D).astype(bf16)
        return 0

    lax.fori_loop(0, N // NR, ln, 0)

    stage3(NB - 1)
    nat0[...] = jnp.dot(pmt[...], nat1[...], preferred_element_type=f32).astype(bf16)
    fg_copy = pltpu.make_async_copy(nat0, fg_o, in_sem.at[0])
    fg_copy.start()
    loop15(lambda i: g2(i).wait_recv())
    t = gg2[...]
    for i in range(15):
        t = t + gg2r[i]
    gg4[...] = t
    for j in (1, 2, 3):
        g3(j).start()

    def done(b, _):
        loop15(lambda i: s3(b, i).wait())
        s3_own(b).wait()
        return 0

    for b in (2, 5):
        for j in (1, 2, 3):
            k3(b, j).wait()
            k1(b, j).wait_send()
        ksib(b).wait_send()
        loop15(lambda i: k2(b, i).wait_send())
        g = b // 3
        gk_o[:, g * 3 * C : (g + 1) * 3 * C] = kgo[g].reshape(32, 3 * C)[0:K]

    lax.fori_loop(0, NB, done, 0)
    lax.fori_loop(0, NB, sent_w, 0)
    for b in (NB - 2, NB - 1):
        sib_send(b).wait_send()
        for j in (1, 2, 3):
            s1(b, j).wait_send()
        loop15(lambda i: s2(b, i).wait_send())
    g1().wait_send()
    loop15(lambda i: g2(i).wait_send())
    for j in (1, 2, 3):
        g3(j).wait()
    gg_o[...] = ((gg4[...] + gg3r[0] + gg3r[1] + gg3r[2]) * root)[0 : D // 128]
    fg_copy.wait()
    mo_copy.wait()


def local(frames, cotangent, w_in, kernel, gain, lengths):
    V, DMA = pltpu.VMEM, pltpu.SemaphoreType.DMA
    far = pl.BlockSpec(memory_space=pl.ANY)
    near = pl.BlockSpec(memory_space=pltpu.VMEM)
    mo, fg, gw, gk, gg = pl.pallas_call(
        body,
        out_shape=[
            jax.ShapeDtypeStruct((N, D), bf16),
            jax.ShapeDtypeStruct((N, D), bf16),
            jax.ShapeDtypeStruct((RB, 2 * D), bf16),
            jax.ShapeDtypeStruct((K, D), f32),
            jax.ShapeDtypeStruct((D // 128, 128), f32),
        ],
        in_specs=[far, far, far, near, near, near],
        out_specs=[far, far, far, near, near],
        scratch_shapes=[
            V((N, D), bf16), V((N, D), bf16), V((N, N), bf16), V((N, N), bf16), V((N, D), bf16), V((N, D), bf16),
            V((N, 1), f32), V((N, 1), f32), V((N, D), bf16), V((D, N), bf16),
            V((NB, 8, RB, C2), bf16), V((NB, N, C2), bf16), V((N, C2), f32),
            V((LT, L + 2 * R, U, 128), f32), V((LT, L + 2 * R, U, 128), f32),
            V((K + 1, 8, 128), f32), V((U, 128), jnp.int32), V((N, D), f32),
            V((4, RB, C2), f32), V((2, 4, RB, C2), bf16), V((NB, 4, RB, C2), bf16),
            V((2, 4, 4, RX, C2), bf16), V((NB, 3, 4, RX, C2), bf16),
            V((2, 4, 4, RX, 128), bf16), V((NB, 15, RX, 128), bf16), V((NB, RX, 128), bf16),
            V((2, 32, 3 * C), f32), V((2, 32, 3 * C), f32), V((2, 4, 8, 3 * C), f32), V((2, 3, 8, 3 * C), f32),
            V((2, 8, 3 * C), f32), V((2, 15, 8, 3 * C), f32), V((2, 4, 8, 3 * C), f32),
            V((8, D), f32), V((16, 128), f32), V((16, 128), f32), V((15, 16, 128), f32),
            V((16, 128), f32), V((3, 16, 128), f32), V((16, 128), f32),
            DMA((2,)), DMA((1,)), DMA((NB, 2)), DMA((NB, 3)), DMA((NB, 3)), DMA((NB, 4)), DMA((NB, 4)),
            DMA((2,)), DMA((NB,)), DMA((2, 3)), DMA((NB, 3)), DMA((2, 15)), DMA((NB, 15)),
            DMA((NB, 15)), DMA((NB, 15)), DMA((NB,)),
            DMA((2,)), DMA((2,)), DMA((2, 3)), DMA((2, 3)), DMA((2, 15)), DMA((2, 15)),
            DMA((2, 3)), DMA((2, 3)), DMA((19,)), DMA((19,)),
        ],
        compiler_params=pltpu.CompilerParams(collective_id=0, has_side_effects=True, vmem_limit_bytes=62 << 20),
    )(
        frames.reshape(N, D),
        cotangent.reshape(N, D),
        w_in,
        kernel,
        gain.reshape(D // 128, 128),
        lengths.reshape(16, 128),
    )
    return mo.reshape(U, L, D), fg.reshape(U, L, D), gw.astype(f32), gk, gg.reshape(D)


def solution(mesh):
    rows = P(("dp", "red"), None, None)
    return jax.shard_map(
        local,
        mesh=mesh,
        in_specs=(rows, rows, P("red", None), P(), P(), P()),
        out_specs=(rows, rows, P("red", None), P(), P()),
        check_vma=False,
    )
```

```python
import functools

import jax
import jax.numpy as jnp
from jax import lax
from jax.experimental import pallas as pl
from jax.experimental.pallas import tpu as pltpu
from jax.sharding import PartitionSpec as P

EPSILON = 1e-05
D = 1536
K = 31
R = K // 2
U = 16
L = 48
N = U * L
C = 256
C2 = 2 * C
NB = D // C
LT = C // 128
T = 8
RB = 192
RX = RB // 4
MESH = pl.DeviceIdType.MESH
f32 = jnp.float32
bf16 = jnp.bfloat16


def sigmoid(x):
    return 0.5 * jnp.tanh(0.5 * x) + 0.5


def aligned(i, n):
    return pl.ds(pl.multiple_of(i, n), n)


def body(
    frames, cot, w, kern, gain, lens,
    mo_o, fg_o, gw_o, gk_o, gg_o,
    nat0, nat1, pm, pmt, fr, up, mean, istd, sc, sct, W, gh, h, glu, gcp, kg, len16, gs,
    own, sibs, sibr, s1s, s1r, s2s, s2r, gwp,
    kgl, kgsr, kg1, kg1r, kg2, kg2r, kgo, ggl, ggr, gg2, gg2r, gg3, gg3r, gg4,
    in_sem, mo_sem, wl_sem, wz_s, wz_r, ws_s, ws_r,
    ss_s, ss_r, s1_s, s1_r, s2_s, s2_r, s3_s, s3_r, s3_l,
    ks_s, ks_r, k1_s, k1_r, k2_s, k2_r, k3_s, k3_r, g_s, g_r,
):
    dp, red = lax.axis_index("dp"), lax.axis_index("red")
    x, y = lax.div(dp, 4), lax.rem(dp, 4)
    z, c = lax.div(red, 2), lax.rem(red, 2)

    def turn(a, d):
        return (a + d) & 3

    def at(ax, ay, az, ac):
        return (ax * 4 + ay, az * 2 + ac)

    sib = at(x, y, z, 1 - c)

    def remote(src, dst, ssem, rsem, dev):
        return pltpu.make_async_remote_copy(
            src_ref=src, dst_ref=dst, send_sem=ssem, recv_sem=rsem, device_id=dev, device_id_type=MESH
        )

    def first(b, d):
        p = lax.rem(b, 2)
        return at(turn(x, d * (1 - p)), turn(y, d * p), z, c)

    def plane(b, d, dz):
        p = lax.rem(b, 2)
        return at(turn(x, d * p), turn(y, d * (1 - p)), turn(z, dz), c)

    def place(b):
        p = lax.rem(b, 2)
        return x * (1 - p) + y * p, x * p + y * (1 - p)

    in0 = pltpu.make_async_copy(frames, nat0, in_sem.at[0])
    in0.start()

    def own_w(b, half):
        return pltpu.make_async_copy(
            w.at[:, aligned(half * D + b * C, C)], W.at[b, red, :, pl.ds(half * C, C)], wl_sem.at[b, half]
        )

    for b in range(NB):
        own_w(b, 0).start()
        own_w(b, 1).start()
    in1 = pltpu.make_async_copy(cot, nat1, in_sem.at[1])
    in1.start()

    barrier = pltpu.get_barrier_semaphore()
    offsets = [
        (i, j, k) for i in range(4) for j in range(4) for k in range(4) if (i, j, k) != (0, 0, 0) and i * j * k == 0
    ]
    pl.semaphore_signal(barrier, inc=1, device_id=sib, device_id_type=MESH)
    for i, j, k in offsets:
        pl.semaphore_signal(barrier, inc=1, device_id=at(turn(x, i), turn(y, j), turn(z, k), c), device_id_type=MESH)
    pl.semaphore_wait(barrier, len(offsets) + 1)

    def wz(b, j):
        return remote(W.at[b, red], W.at[b, red], wz_s.at[b, j - 1], wz_r.at[b, j - 1], at(x, y, turn(z, j), c))

    def wsib(b, j):
        held = turn(z, 4 - j) * 2 + c
        return remote(W.at[b, held], W.at[b, held], ws_s.at[b, j], ws_r.at[b, j], sib)

    def send_w(b, _):
        own_w(b, 0).wait()
        own_w(b, 1).wait()
        for j in (1, 3, 2):
            wz(b, j).start()
        wsib(b, 0).start()
        return 0

    def forward_w(b):
        for j in (1, 3, 2):
            wz(b, j).wait_recv()
            wsib(b, j).start()

    def arrived_w(b):
        for j in range(4):
            wsib(b, j).wait_recv()

    def sent_w(b, _):
        for j in (1, 2, 3):
            wz(b, j).wait_send()
        for j in range(4):
            wsib(b, j).wait_send()
        return 0

    lax.fori_loop(0, NB, send_w, 0)

    r0 = lax.broadcasted_iota(jnp.int32, (N, N), 0)
    r1 = lax.broadcasted_iota(jnp.int32, (N, N), 1)
    pm[...] = jnp.where(((r0 & 15) * L + (r0 >> 4)) == r1, 1.0, 0.0).astype(bf16)
    pmt[...] = jnp.where(((r1 & 15) * L + (r1 >> 4)) == r0, 1.0, 0.0).astype(bf16)
    me = dp * 8 + red
    row = lens[pl.ds(lax.div(me, 8), 1), :]
    sub = lax.broadcasted_iota(jnp.int32, (U, 128), 0)
    lane = lax.broadcasted_iota(jnp.int32, (U, 128), 1)
    mine = jnp.where(lane == sub + lax.rem(me, 8) * U, row, 0)
    len16[...] = jnp.broadcast_to(jnp.sum(mine, axis=1, keepdims=True), (U, 128))
    every = jnp.sum(jnp.sum(lens[...], axis=0, keepdims=True), axis=1, keepdims=True)
    root = lax.rsqrt(every.astype(f32))
    glu[...] = jnp.zeros_like(glu)
    gcp[...] = jnp.zeros_like(gcp)
    gg3[...] = jnp.zeros_like(gg3)

    def live(t0, n, lanes):
        t = lax.broadcasted_iota(jnp.int32, (n, U, lanes), 0) + t0
        return t < len16[:, :lanes][None]

    in0.wait()
    PR = 256

    def perm_frames(i, _):
        rows = aligned(i * PR, PR)
        fr[rows, :] = jnp.dot(pm[rows, :], nat0[...], preferred_element_type=f32).astype(bf16)
        return 0

    lax.fori_loop(0, N // PR, perm_frames, 0)

    gain_row = jnp.concatenate([gain[q : q + 1, :] for q in range(D // 128)], axis=1)

    def norm(i, _):
        NR = 128
        rows = aligned(i * NR, NR)
        v = fr[rows, :].astype(f32)
        m = jnp.mean(v, axis=-1, keepdims=True)
        cen = v - m
        s = lax.rsqrt(jnp.mean(cen * cen, axis=-1, keepdims=True) + EPSILON)
        mean[rows, :] = m
        istd[rows, :] = s
        scaled = cen * s * gain_row
        sc[rows, :] = scaled.astype(bf16)
        turned = scaled.T.astype(bf16)
        for q in range(8):
            other = lax.rem(c + q % 2, 2)
            dst = other * (4 * RB) + (q // 2) * RB
            sct[aligned_rows(dst, RB), rows] = turned[q * RB : (q + 1) * RB, :]
        return 0

    def aligned_rows(i, n):
        return pl.ds(pl.multiple_of(i, 64), n)

    lax.fori_loop(0, N // 128, norm, 0)
    in1.wait()

    def perm_cot(i, _):
        rows = aligned(i * PR, PR)
        v = jnp.dot(pm[rows, :], nat1[...], preferred_element_type=f32).reshape(PR // U, U, D)
        up[rows, :] = jnp.where(live(i * (PR // U), PR // U, 1), v, 0.0).reshape(PR, D).astype(bf16)
        return 0

    lax.fori_loop(0, N // PR, perm_cot, 0)

    def sib_send(b):
        return remote(sibs.at[lax.rem(b, 2)], sibr.at[b], ss_s.at[lax.rem(b, 2)], ss_r.at[b], sib)

    def ksib(b):
        return remote(kgl.at[lax.div(b, 3)], kgsr.at[lax.div(b, 3)], ks_s.at[lax.div(b, 3)], ks_r.at[lax.div(b, 3)], sib)

    def s1(b, j):
        p = lax.rem(b, 2)
        f, _ = place(b)
        return remote(s1s.at[p, turn(f, j)], s1r.at[b, j - 1], s1_s.at[p, j - 1], s1_r.at[b, j - 1], first(b, j))

    def k1(b, j):
        f, _ = place(b)
        g = lax.div(b, 3)
        return remote(kg1.at[g, turn(f, j)], kg1r.at[g, j - 1], k1_s.at[g, j - 1], k1_r.at[g, j - 1], first(b, j))

    def s2(b, i):
        p = lax.rem(b, 2)
        _, s = place(b)
        d, dz = i // 4, i % 4
        return remote(
            s2s.at[p, turn(s, d), turn(z, dz)], s2r.at[b, i - 1], s2_s.at[p, i - 1], s2_r.at[b, i - 1], plane(b, d, dz)
        )

    def k2(b, i):
        d, dz = i // 4, i % 4
        g = lax.div(b, 3)
        return remote(kg2.at[g], kg2r.at[g, i - 1], k2_s.at[g, i - 1], k2_r.at[g, i - 1], plane(b, d, dz))

    def piece(b):
        f, s = place(b)
        return gw_o.at[aligned(f * RX, RX), aligned(lax.div(s, 2) * D + b * C + lax.rem(s, 2) * 128, 128)]

    def s3(b, i):
        dev = at(turn(x, i // 4), turn(y, i % 4), z, c)
        return remote(gwp.at[b], piece(b), s3_s.at[b, i - 1], s3_r.at[b, i - 1], dev)

    def s3_own(b):
        return pltpu.make_async_copy(gwp.at[b], piece(b), s3_l.at[b])

    def k3(b, j):
        f, _ = place(b)
        g = lax.div(b, 3)
        return remote(kgo.at[g, f], kgo.at[g, f], k3_s.at[g, j - 1], k3_r.at[g, j - 1], first(b, j))

    def loop15(fn):
        for i in range(1, 16):
            fn(i)

    def stage1(b):
        p = lax.rem(b, 2)
        sib_send(b).wait_recv()

        @pl.when(b >= 2)
        def _():
            for j in (1, 2, 3):
                s1(b - 2, j).wait_send()

        def add(q, _):
            v = own[q] + sibr[b, q].astype(f32)
            for f in range(4):
                s1s[p, f, q] = v[f * RX : (f + 1) * RX].astype(bf16)
            return 0

        lax.fori_loop(0, 4, add, 0)
        for j in (1, 3, 2):
            s1(b, j).start()

        @pl.when(lax.rem(b, 3) == 2)
        def _():
            g = lax.div(b, 3)
            ksib(b).wait_recv()
            t = kgl[g] + kgsr[g]
            for f in range(4):
                kg1[g, f] = t[f * 8 : (f + 1) * 8]
            for j in (1, 3, 2):
                k1(b, j).start()

    def stage2(b):
        p = lax.rem(b, 2)
        f, _ = place(b)
        for j in (1, 2, 3):
            s1(b, j).wait_recv()

        @pl.when(b >= 2)
        def _():
            loop15(lambda i: s2(b - 2, i).wait_send())

        def add(q, _):
            v = s1s[p, f, q].astype(f32)
            for j in range(3):
                v = v + s1r[b, j, q].astype(f32)
            for s in range(4):
                s2s[p, s, q] = v[:, s * 128 : (s + 1) * 128].astype(bf16)
            return 0

        lax.fori_loop(0, 4, add, 0)
        loop15(lambda i: s2(b, i).start())

        @pl.when(lax.rem(b, 3) == 2)
        def _():
            g = lax.div(b, 3)
            for j in (1, 2, 3):
                k1(b, j).wait_recv()
            kg2[g] = kg1[g, f] + kg1r[g, 0] + kg1r[g, 1] + kg1r[g, 2]
            loop15(lambda i: k2(b, i).start())

    def stage3(b):
        p = lax.rem(b, 2)
        f, s = place(b)
        loop15(lambda i: s2(b, i).wait_recv())
        v = s2s[p, s, z].astype(f32)
        for i in range(15):
            v = v + s2r[b, i].astype(f32)
        gwp[b] = (v * root).astype(bf16)
        loop15(lambda i: s3(b, i).start())
        s3_own(b).start()

        @pl.when(lax.rem(b, 3) == 2)
        def _():
            g = lax.div(b, 3)
            loop15(lambda i: k2(b, i).wait_recv())
            t = kg2[g]
            for i in range(15):
                t = t + kg2r[g, i]
            kgo[g, f] = t * root
            for j in (1, 2, 3):
                k3(b, j).start()

    def put_taps(b, lt):
        kgl[lax.div(b, 3), :, aligned(lax.rem(b, 3) * C + lt * 128, 128)] = jnp.sum(kg[...], axis=1)

    def trimmed(step, at_start, at_end):
        step(0, at_start)

        def inner(i, _):
            step(i, range(K))
            return 0

        lax.fori_loop(1, L // T - 1, inner, 0)
        step(L // T - 1, at_end)

    def block(b, _):
        forward_first = b == 0

        @pl.when(forward_first)
        def _():
            forward_w(b)

        arrived_w(b)

        h[...] = jnp.dot(sc[...], W[b].reshape(D, C2), preferred_element_type=f32)

        @pl.when(b >= 4)
        def _():
            stage3(b - 4)

        @pl.when(b >= 3)
        def _():
            stage2(b - 3)

        @pl.when(b >= 1)
        def _():
            stage1(b - 1)

        for lt in range(LT):
            vl = slice(lt * 128, (lt + 1) * 128)
            gl = slice(C + lt * 128, C + (lt + 1) * 128)
            cl = aligned(b * C + lt * 128, 128)

            def gate(i, _):
                rows = aligned(i * (T * U), T * U)
                s = sigmoid(h[rows, gl])
                h[rows, gl] = s
                out = jnp.where(live(i * T, T, 128), (h[rows, vl] * s).reshape(T, U, 128), 0.0)
                glu[lt, pl.ds(i * T + R, T)] = out
                return 0

            lax.fori_loop(0, L // T, gate, 0)
            kg[...] = jnp.zeros_like(kg)

            def forward(i, taps):
                t0 = i * T
                rows = aligned(i * (T * U), T * U)
                acc = jnp.zeros((T, U, 128), f32)
                for k in taps:
                    acc = acc + kern[k : k + 1, cl][None] * glu[lt, pl.ds(t0 + k, T)]
                s = sigmoid(acc)
                swish = acc * s
                out = jnp.where(live(t0, T, 128), fr[rows, cl].astype(f32).reshape(T, U, 128) + swish, 0.0)
                nat0[rows, cl] = out.reshape(T * U, 128).astype(bf16)
                gc = up[rows, cl].astype(f32).reshape(T, U, 128) * (s + swish * (1.0 - s))
                gcp[lt, pl.ds(t0 + R, T)] = gc
                for k in taps:
                    p = jnp.sum(gc * glu[lt, pl.ds(t0 + k, T)], axis=0)
                    kg[k] += p[0:8] + p[8:16]

            trimmed(forward, range(T, K), range(K - T))
            put_taps(b, lt)

            def backward(i, taps):
                t0 = i * T
                rows = aligned(i * (T * U), T * U)
                acc = jnp.zeros((T, U, 128), f32)
                for k in taps:
                    acc = acc + kern[k : k + 1, cl][None] * gcp[lt, pl.ds(t0 + (K - 1) - k, T)]
                dg = jnp.where(live(t0, T, 128), acc, 0.0)
                s = h[rows, gl].reshape(T, U, 128)
                gh[b, rows, vl] = (dg * s).reshape(T * U, 128).astype(bf16)
                gate_part = dg * glu[lt, pl.ds(t0 + R, T)] * (1.0 - s)
                gh[b, rows, gl] = gate_part.reshape(T * U, 128).astype(bf16)

            trimmed(backward, range(K - T), range(T, K))

        @pl.when(b + 1 < NB)
        def _():
            forward_w(b + 1)

        @pl.when(b >= 2)
        def _():
            sib_send(b - 2).wait_send()

        g = jnp.dot(sct[4 * RB :, :], gh[b], preferred_element_type=f32).astype(bf16)
        sibs[lax.rem(b, 2)] = g.reshape(4, RB, C2)
        sib_send(b).start()

        @pl.when(lax.rem(b, 3) == 2)
        def _():
            ksib(b).start()

        own[...] = jnp.dot(sct[: 4 * RB, :], gh[b], preferred_element_type=f32).reshape(4, RB, C2)
        return 0

    lax.fori_loop(0, NB, block, 0)

    stage2(NB - 3)
    stage1(NB - 1)
    sc[...] = jnp.dot(pmt[...], nat0[...], preferred_element_type=f32).astype(bf16)
    mo_copy = pltpu.make_async_copy(sc, mo_o, mo_sem.at[0])
    mo_copy.start()
    stage3(NB - 4)
    stage2(NB - 2)
    ggl[...] = jnp.zeros_like(ggl)

    def g1():
        return remote(gg3, ggr, g_s.at[18], g_r.at[18], sib)

    def g2(i):
        return remote(gg2, gg2r.at[i - 1], g_s.at[i - 1], g_r.at[i - 1], plane(0, i // 4, i % 4))

    def g3(j):
        return remote(gg4, gg3r.at[j - 1], g_s.at[14 + j], g_r.at[14 + j], first(0, j))

    def acc(b, _):
        p = lax.dot_general(gh[b], W[b].reshape(D, C2), (((1,), (1,)), ((), ())), preferred_element_type=f32)

        @pl.when(b == 0)
        def _():
            gs[...] = p

        @pl.when(b > 0)
        def _():
            gs[...] += p

        @pl.when(b == 1)
        def _():
            stage3(NB - 3)

        @pl.when(b == 4)
        def _():
            stage3(NB - 2)

        return 0

    lax.fori_loop(0, NB, acc, 0)
    NR = 64

    def normed(r):
        return (fr[r, :].astype(f32) - mean[r, :]) * istd[r, :]

    def gain_part(j, _):
        r = aligned(j * NR, NR)
        ggl[...] += jnp.sum((gs[r, :] * normed(r)).reshape(NR // 8, 8, D), axis=0)
        return 0

    lax.fori_loop(0, N // NR, gain_part, 0)
    total = jnp.sum(ggl[...], axis=0, keepdims=True)
    for q in range(D // 128):
        gg3[q : q + 1, :] = total[:, q * 128 : (q + 1) * 128]
    g1().start()

    def ln(j, _):
        @pl.when(j == 3)
        def _():
            g1().wait_recv()
            gg2[...] = gg3[...] + ggr[...]
            loop15(lambda i: g2(i).start())

        @pl.when(j == 4)
        def _():
            stage2(NB - 1)

        r = aligned(j * NR, NR)
        s = istd[r, :]
        nm = normed(r)
        g = gs[r, :] * gain_row
        m1 = jnp.mean(g, axis=-1, keepdims=True)
        m2 = jnp.mean(g * nm, axis=-1, keepdims=True)
        o = up[r, :].astype(f32) + s * (g - m1 - nm * m2)
        lv = live(j * (NR // U), NR // U, 1)
        nat1[r, :] = jnp.where(lv, o.reshape(NR // U, U, D), 0.0).reshape(NR, D).astype(bf16)
        return 0

    lax.fori_loop(0, N // NR, ln, 0)

    nat0[...] = jnp.dot(pmt[...], nat1[...], preferred_element_type=f32).astype(bf16)
    fg_copy = pltpu.make_async_copy(nat0, fg_o, in_sem.at[0])
    fg_copy.start()
    stage3(NB - 1)
    loop15(lambda i: g2(i).wait_recv())
    t = gg2[...]
    for i in range(15):
        t = t + gg2r[i]
    gg4[...] = t
    for j in (1, 2, 3):
        g3(j).start()

    def done(b, _):
        loop15(lambda i: s3(b, i).wait())
        s3_own(b).wait()
        return 0

    for b in (2, 5):
        for j in (1, 2, 3):
            k3(b, j).wait()
            k1(b, j).wait_send()
        ksib(b).wait_send()
        loop15(lambda i: k2(b, i).wait_send())
        g = b // 3
        gk_o[:, g * 3 * C : (g + 1) * 3 * C] = kgo[g].reshape(32, 3 * C)[0:K]

    lax.fori_loop(0, NB, done, 0)
    lax.fori_loop(0, NB, sent_w, 0)
    for b in (NB - 2, NB - 1):
        sib_send(b).wait_send()
        for j in (1, 2, 3):
            s1(b, j).wait_send()
        loop15(lambda i: s2(b, i).wait_send())
    g1().wait_send()
    loop15(lambda i: g2(i).wait_send())
    for j in (1, 2, 3):
        g3(j).wait()
    gg_o[...] = ((gg4[...] + gg3r[0] + gg3r[1] + gg3r[2]) * root)[0 : D // 128]
    fg_copy.wait()
    mo_copy.wait()


def local(frames, cotangent, w_in, kernel, gain, lengths):
    V, DMA = pltpu.VMEM, pltpu.SemaphoreType.DMA
    far = pl.BlockSpec(memory_space=pl.ANY)
    near = pl.BlockSpec(memory_space=pltpu.VMEM)
    mo, fg, gw, gk, gg = pl.pallas_call(
        body,
        out_shape=[
            jax.ShapeDtypeStruct((N, D), bf16),
            jax.ShapeDtypeStruct((N, D), bf16),
            jax.ShapeDtypeStruct((RB, 2 * D), bf16),
            jax.ShapeDtypeStruct((K, D), f32),
            jax.ShapeDtypeStruct((D // 128, 128), f32),
        ],
        in_specs=[far, far, far, near, near, near],
        out_specs=[far, far, far, near, near],
        scratch_shapes=[
            V((N, D), bf16), V((N, D), bf16), V((N, N), bf16), V((N, N), bf16), V((N, D), bf16), V((N, D), bf16),
            V((N, 1), f32), V((N, 1), f32), V((N, D), bf16), V((D, N), bf16),
            V((NB, 8, RB, C2), bf16), V((NB, N, C2), bf16), V((N, C2), f32),
            V((LT, L + 2 * R, U, 128), f32), V((LT, L + 2 * R, U, 128), f32),
            V((K + 1, 8, 128), f32), V((U, 128), jnp.int32), V((N, D), f32),
            V((4, RB, C2), f32), V((2, 4, RB, C2), bf16), V((NB, 4, RB, C2), bf16),
            V((2, 4, 4, RX, C2), bf16), V((NB, 3, 4, RX, C2), bf16),
            V((2, 4, 4, RX, 128), bf16), V((NB, 15, RX, 128), bf16), V((NB, RX, 128), bf16),
            V((2, 32, 3 * C), f32), V((2, 32, 3 * C), f32), V((2, 4, 8, 3 * C), f32), V((2, 3, 8, 3 * C), f32),
            V((2, 8, 3 * C), f32), V((2, 15, 8, 3 * C), f32), V((2, 4, 8, 3 * C), f32),
            V((8, D), f32), V((16, 128), f32), V((16, 128), f32), V((15, 16, 128), f32),
            V((16, 128), f32), V((3, 16, 128), f32), V((16, 128), f32),
            DMA((2,)), DMA((1,)), DMA((NB, 2)), DMA((NB, 3)), DMA((NB, 3)), DMA((NB, 4)), DMA((NB, 4)),
            DMA((2,)), DMA((NB,)), DMA((2, 3)), DMA((NB, 3)), DMA((2, 15)), DMA((NB, 15)),
            DMA((NB, 15)), DMA((NB, 15)), DMA((NB,)),
            DMA((2,)), DMA((2,)), DMA((2, 3)), DMA((2, 3)), DMA((2, 15)), DMA((2, 15)),
            DMA((2, 3)), DMA((2, 3)), DMA((19,)), DMA((19,)),
        ],
        compiler_params=pltpu.CompilerParams(collective_id=0, has_side_effects=True, vmem_limit_bytes=62 << 20),
    )(
        frames.reshape(N, D),
        cotangent.reshape(N, D),
        w_in,
        kernel,
        gain.reshape(D // 128, 128),
        lengths.reshape(16, 128),
    )
    return mo.reshape(U, L, D), fg.reshape(U, L, D), gw.astype(f32), gk, gg.reshape(D)


def solution(mesh):
    rows = P(("dp", "red"), None, None)
    return jax.shard_map(
        local,
        mesh=mesh,
        in_specs=(rows, rows, P("red", None), P(), P(), P()),
        out_specs=(rows, rows, P("red", None), P(), P()),
        check_vma=False,
    )
```
